256 devices in a mesh: prow: 8 (over x, core), pcol: 32 (over z, y).
Axes of the slice: x: 4, y: 4, z: 8, core: 2. Of those that a mesh axis runs over, the one named last changes fastest.
Arguments:
- matrix: bfloat16 [4, 8, 512, 1, 32, 512], P(None, 'prow', None, None, 'pcol'), may hold values from -6 to 6
- upper_inv: bfloat16 [2, 512, 512], replicated, may hold values from -4 to 4
- lower_inv: bfloat16 [2, 512, 512], replicated, may hold values from -4 to 4
- solution: bfloat16 [1, 32, 512], P(None, 'pcol'), may hold values from -0.046875 to 0.046875
- right_side: float32 [4, 8, 512], P(None, 'prow'), may hold values from -6 to 6
- diagonal_block_inverses: bfloat16 [1, 8, 512, 512], P(None, 'prow'), may hold values from -0.009765625 to 0.009765625
Outputs:
- updated: bfloat16 [4, 8, 512, 1, 32, 512], P(None, 'prow', None, None, 'pcol')
- residual: float32 [4, 8, 512], P(None, 'prow')
- precond: float32 [8, 512], replicated
The draws below stay inside these ranges and needn't reach their ends.
All inputs are finite; a program needn't handle non-finite values.
Results may differ from the reference program's by a relative error of at most 0.0085.
Values may be sent and summed in bfloat16 or wider, within the bound.
A program may use at most 128 MiB of HBM per device.

```python
import jax
import jax.numpy as jnp
from jax import lax

N = 16384
PANEL_WIDTH = 512
PANELS = 2
PROW_BLOCK_ROWS = 1
RB = 4
CB = 1
SOLVE_BLOCK_ROWS = 8
N_PROW = 8
N_PCOL = 32


def unit_entries(key, salt):
    folded = jax.random.fold_in(key, salt)
    entries = jax.random.normal(folded, (PANELS, PANEL_WIDTH, PANEL_WIDTH), jnp.float32)
    return jnp.clip(entries, -4.0, 4.0)


def draw_upper_inv(key, part):
    entries = unit_entries(key, 11)
    column_ids = jnp.arange(PANEL_WIDTH, dtype=jnp.float32) + 1.0
    column_factor = 1.0 / jnp.sqrt(column_ids * PANEL_WIDTH)
    return (entries * column_factor[None, None, :]).astype(jnp.bfloat16)


def draw_lower_inv(key, part):
    entries = unit_entries(key, 23)
    row_ids = jnp.arange(PANEL_WIDTH, dtype=jnp.float32) + 1.0
    row_factor = 1.0 / jnp.sqrt(row_ids)
    return (entries * row_factor[None, :, None]).astype(jnp.bfloat16)


def steps_of(rng, shape, cuts, least, largest):
    def one(position, parts):
        steps = jax.random.uniform(jax.random.fold_in(jax.random.fold_in(rng, 6), position), (parts,), jnp.float32, least / len(cuts), largest / len(cuts))
        return jnp.repeat(jnp.exp(steps), shape[position] // parts).reshape((-1,) + (1,) * (len(shape) - position - 1))

    loudness = one(*cuts[0])
    for cut in cuts[1:]:
        loudness = loudness * one(*cut)
    return loudness


def noise(rng, extent, spread, bound, shards=(), kind=jnp.bfloat16):
    values = spread * jax.random.normal(rng, extent, jnp.float32)
    if shards:
        values = values * steps_of(rng, extent, shards, -0.22, 0.18)
    return jnp.clip(values, -bound, bound).astype(kind)


def setup_inputs(seed: int = 0) -> dict:
    seeds = jax.random.split(jax.random.key(seed), 7)
    return {
        "matrix": noise(seeds[0], (RB, N_PROW, PANEL_WIDTH, CB, N_PCOL, PANEL_WIDTH), 1.0, 6.0, ((1, 8), (4, 32))),
        "upper_inv": draw_upper_inv(jax.random.fold_in(seeds[6], 71), 0),
        "lower_inv": draw_lower_inv(jax.random.fold_in(seeds[6], 71), 0),
        "solution": noise(seeds[3], (CB, N_PCOL, PANEL_WIDTH), N ** -0.5, 0.046875, ((1, 32),)),
        "right_side": noise(seeds[4], (RB, N_PROW, PANEL_WIDTH), 1.0, 6.0, ((1, 8),), jnp.float32),
        "diagonal_block_inverses": noise(seeds[5], (PROW_BLOCK_ROWS, N_PROW, PANEL_WIDTH, PANEL_WIDTH), (PANEL_WIDTH * PANEL_WIDTH * SOLVE_BLOCK_ROWS // 6) ** -0.5, 0.009765625, ((1, 8),)),
    }


def reference(matrix, upper_inv, lower_inv, solution, right_side, diagonal_block_inverses):
    base_matrix = matrix.reshape(N, N)
    current = base_matrix
    for section in range(PANELS):
        upper_tri = jnp.triu(upper_inv[section])
        lower_tri = jnp.tril(lower_inv[section])
        column = current[:, section * PANEL_WIDTH:(section + 1) * PANEL_WIDTH]
        row_band = current[section * PANEL_WIDTH:(section + 1) * PANEL_WIDTH, :]
        left_panel = jnp.dot(column, upper_tri, preferred_element_type=jnp.float32).astype(jnp.bfloat16)
        top_panel = jnp.dot(lower_tri, row_band, preferred_element_type=jnp.float32).astype(jnp.bfloat16)
        current = (current.astype(jnp.float32) - jnp.dot(left_panel, top_panel, preferred_element_type=jnp.float32)).astype(jnp.bfloat16)
    updated = current.reshape(matrix.shape)
    residual = right_side.reshape(N) - jnp.dot(base_matrix, solution.reshape(N), preferred_element_type=jnp.float32)
    res_blocks = residual.reshape(N // PANEL_WIDTH, PANEL_WIDTH)
    inverses = diagonal_block_inverses.reshape(SOLVE_BLOCK_ROWS, PANEL_WIDTH, PANEL_WIDTH)
    leading = base_matrix[:SOLVE_BLOCK_ROWS * PANEL_WIDTH, :SOLVE_BLOCK_ROWS * PANEL_WIDTH]

    def carry_forward(blk_id, state):
        rounded, solved = state
        row_piece = lax.dynamic_slice_in_dim(leading, blk_id * PANEL_WIDTH, PANEL_WIDTH, 0)
        pending = jnp.dot(row_piece, rounded.reshape(SOLVE_BLOCK_ROWS * PANEL_WIDTH), preferred_element_type=jnp.float32)
        res_block = lax.dynamic_slice_in_dim(res_blocks, blk_id, 1, 0)[0]
        inv_block = lax.dynamic_slice_in_dim(inverses, blk_id, 1, 0)[0].astype(jnp.float32)
        new_value = jnp.dot(inv_block, res_block - pending, precision=lax.Precision.HIGHEST)
        solved = lax.dynamic_update_slice_in_dim(solved, new_value[None], blk_id, 0)
        rounded = lax.dynamic_update_slice_in_dim(rounded, new_value.astype(jnp.bfloat16)[None], blk_id, 0)
        return rounded, solved

    start = (jnp.zeros((SOLVE_BLOCK_ROWS, PANEL_WIDTH), jnp.bfloat16), jnp.zeros((SOLVE_BLOCK_ROWS, PANEL_WIDTH), jnp.float32))
    precond = lax.fori_loop(0, SOLVE_BLOCK_ROWS, carry_forward, start)[1]
    return updated, residual.reshape(right_side.shape), precond
```

```python
import jax
import jax.numpy as jnp
from jax import lax
from jax.experimental import pallas as pl
from jax.experimental.pallas import tpu as pltpu
from jax.sharding import PartitionSpec as P

MESH = pl.DeviceIdType.MESH
B = 512
CH = 64
NCD = B // CH
NCC = 64 // CH
NC = NCD + NCC
NPOS = 4
LAG_NUM, LAG_DEN = 3, 2
MAXD = 7
DIRS = ((1, 0), (-1, 0), (0, 1), (0, -1))
TREES = (
    (1, 29, 33, 48, 48, 39, 48, 96, 64, 55, 65, 88, 80, 71, 81, 96, 96, 83, 97, 112, 80, 66, 81, 96, 64, 59, 73, 84, 48, 43, 48, 96),
    (4, 80, 72, 48, 22, 72, 56, 42, 39, 56, 96, 48, 55, 64, 92, 70, 69, 84, 100, 84, 84, 100, 112, 100, 100, 112, 96, 112, 112, 96, 91, 96),
    (8, 80, 68, 48, 112, 96, 87, 96, 104, 112, 96, 112, 88, 104, 112, 104, 74, 88, 104, 90, 59, 73, 84, 64, 43, 52, 96, 48, 26, 68, 52, 38),
    (2, 48, 34, 30, 49, 64, 80, 37, 64, 80, 78, 55, 80, 96, 82, 65, 96, 112, 98, 81, 80, 96, 90, 75, 64, 80, 70, 59, 49, 64, 80, 41),
)
ROOT_DIR = (0, 2, 3, 1)
f32, bf16 = jnp.float32, jnp.bfloat16


def lag(depth):
    return depth * LAG_NUM // LAG_DEN


def dot(a, b):
    return jnp.dot(a, b, preferred_element_type=f32)


def dot_t(a, b):
    return lax.dot_general(a, b, (((1,), (1,)), ((), ())), preferred_element_type=f32)


def row_of(c):
    return jnp.concatenate([c[m : m + 1, :] for m in range(4)], axis=1)


def kernel(
    a_hbm, u_hbm, l_hbm, sol_ref, rhs_ref, inv_hbm,
    out_hbm, res_ref, pre_ref,
    a_v, strm, u_v, l_v, inv_v, chb, xb, comf, w_v, v_f, ry, rz, xs, acc, out_v,
    s_loc, s_out, s_send, s_recv, s_xsend, s_prim, s_oth, s_comsend, s_comx,
    s_blks, s_blkr, s_rys, s_ryr, s_rzs, s_rzr, s_xss, s_xsr, s_fs, s_fz, s_fy, s_cs, s_cr,
):
    p = lax.axis_index("prow")
    q = lax.axis_index("pcol")
    core = p % 2
    y, z = q % 4, q // 4
    is_q = q == 0

    def at(dy, dz):
        return ((z + dz + 8) % 8) * 4 + (y + dy + 4) % 4

    def rcopy(src, dst, ss, rs, dev):
        return pltpu.make_async_remote_copy(
            src_ref=src, dst_ref=dst, send_sem=ss, recv_sem=rs, device_id=dev, device_id_type=MESH
        )

    ld_a = pltpu.make_async_copy(a_hbm, a_v, s_loc.at[0])
    ld_u = pltpu.make_async_copy(u_hbm, u_v, s_loc.at[1])
    ld_l = pltpu.make_async_copy(l_hbm, l_v, s_loc.at[2])
    ld_i = pltpu.make_async_copy(inv_hbm, inv_v, s_loc.at[3])
    ld_a.start()
    for r in range(2):
        pl.when(q == r)(lambda r=r: pltpu.make_async_copy(a_hbm, strm.at[r, pl.ds(0, 4 * B)], s_loc.at[4]).start())
    src_com = (p + q) == 1

    def com_own():
        return pltpu.make_async_copy(
            a_hbm.at[pl.ds(pl.multiple_of(256 * core, 256), 256)], strm.at[q, pl.ds(4 * B, 256)], s_loc.at[5]
        )

    pl.when(src_com)(lambda: com_own().start())

    def xb_own():
        return pltpu.make_async_copy(a_hbm.at[pl.ds(0, B)], xb.at[core], s_loc.at[6])

    pl.when(p < 2)(lambda: xb_own().start())
    ld_u.start()
    ld_l.start()
    ld_i.start()

    bar = pltpu.get_barrier_semaphore()
    zm = [at(0, o) for o in range(1, 8)]
    ym = [at(o, 0) for o in range(1, 4)]
    pm = [(p + o) % 8 for o in range(1, 8)]
    for o in (3, 4, 2, 5, 1, 6, 0):
        pl.semaphore_signal(bar, inc=1, device_id=(p, zm[o]), device_id_type=MESH)
    for d in pm:
        pl.semaphore_signal(bar, inc=1, device_id=(d, q), device_id_type=MESH)
    for d in ym:
        pl.semaphore_signal(bar, inc=1, device_id=(p, d), device_id_type=MESH)

    @pl.when((q == 5) | (q == 6))
    def _():
        pl.semaphore_signal(bar, inc=1, device_id=(p, 0), device_id_type=MESH)

    @pl.when(is_q)
    def _():
        for d in (5, 6):
            pl.semaphore_signal(bar, inc=1, device_id=(p, d), device_id_type=MESH)

    ld_a.wait()
    sol8 = jnp.broadcast_to(sol_ref[...], (16, B))
    for i in range(4):
        part = dot_t(sol8, a_v[i * B : (i + 1) * B, :])
        for m in range(4):
            ry[y, 4 * i + m : 4 * i + m + 1, :] = part[0:1, 128 * m : 128 * (m + 1)]
    info = []
    for r in range(2):
        rel = z * 4 + (y + 4 - r) % 4
        word = jnp.int32(0)
        for k in range(32):
            packed = sum(TREES[t][k] << (7 * t) for t in range(4))
            word = jnp.where(rel == k, jnp.int32(packed), word)
        for t in range(4):
            v = (word // (128**t)) % 128
            dep, mask = v // 16, v % 16
            info.append((r, t, dep * LAG_NUM // LAG_DEN, [(mask // (1 << d)) % 2 for d in range(4)]))
    nbr = [at(dy, dz) for dy, dz in DIRS]
    for r in range(2):
        pl.when(q == r)(lambda r=r: pltpu.make_async_copy(a_hbm, strm.at[r, pl.ds(0, 4 * B)], s_loc.at[4]).wait())
    pl.semaphore_wait(bar, 17 + jnp.where(is_q, 2, jnp.where((q == 5) | (q == 6), 1, 0)))

    def rows(t, n):
        off = jnp.where(
            n < NPOS,
            B * t + CH * n,
            jnp.where(n < NPOS + NCC, 4 * B + 64 * t + CH * (n - NPOS), B * t + CH * (n - NCC)),
        )
        return pl.ds(pl.multiple_of(off, CH), CH)

    def hop(r, t, n, d):
        part = strm.at[r, rows(t, n)]
        return rcopy(part, part, s_send.at[r, t, d], s_recv.at[r, t, n], (p, nbr[d]))

    def inject(lo, hi):
        for r in range(2):

            @pl.when(q == r)
            def _():
                def one(n, c):
                    for t in range(4):
                        hop(r, t, n, ROOT_DIR[t]).start()
                    return c

                lax.fori_loop(lo, hi, one, 0)

    def ry_copy(o):
        return rcopy(ry.at[y], ry.at[y], s_rys.at[o], s_ryr.at[y], (p, ym[o]))

    for o in range(3):
        ry_copy(o).start()
    inject(0, NPOS)

    def com_copy(o):
        half = (pm[o]) % 2
        return rcopy(
            a_v.at[pl.ds(pl.multiple_of(256 * half, 256), 256)], strm.at[q, pl.ds(4 * B, 256)],
            s_comsend.at[o], s_comx, (pm[o], q),
        )

    @pl.when(src_com)
    def _():
        for o in (0, 1, 6, 5, 2, 4, 3):
            com_copy(o).start()
        com_own().wait()

    def blk_copy(j):
        return rcopy(a_v.at[pl.ds(0, B)], chb.at[j - 1], s_blks, s_blkr.at[j - 1], (p, 0))

    for j in range(1, 7):
        pl.when((q == j) & (p > j))(lambda j=j: blk_copy(j).start())

    def xb_copy(o):
        return rcopy(xb.at[core], xb.at[core], s_xsend.at[o], s_prim, (2 * (o + 1) + core, q))

    def xb_pair():
        return rcopy(xb.at[core], xb.at[core], s_xsend.at[3], s_oth, (p + 1 - 2 * core, q))

    @pl.when(p < 2)
    def _():
        xb_own().wait()
        xb_pair().start()
        for o in (0, 2, 1):
            xb_copy(o).start()

    def ticks(lo, hi):
        def one(k, c):
            for r, t, lg, kids in info:
                n = k - lg

                @pl.when((n >= 0) & (n < NC) & (q != r))
                def _():
                    hop(r, t, n, 0).wait_recv()
                    for d in range(4):
                        pl.when(kids[d] == 1)(lambda d=d: hop(r, t, n, d).start())

            return c

        lax.fori_loop(lo, hi, one, 0)

    def rz_copy(o):
        return rcopy(rz.at[z], rz.at[z], s_rzs.at[o], s_rzr.at[z], (p, zm[o]))

    def ev_y():
        for o in range(1, 4):
            src = (y + o) % 4
            rcopy(ry.at[src], ry.at[src], s_rys.at[0], s_ryr.at[src], (p, ym[0])).wait_recv()
        rz[z] = ((ry[0] + ry[1]) + (ry[2] + ry[3]))
        for o in (3, 4, 2, 5, 1, 6, 0):
            rz_copy(o).start()

    def ev_z():
        for o in range(1, 8):
            src = (z + o) % 8
            rcopy(rz.at[src], rz.at[src], s_rzs.at[0], s_rzr.at[src], (p, zm[0])).wait_recv()
        tot = rz[0]
        for k in range(1, 8):
            tot = tot + rz[k]
        for i in range(4):
            res_ref[i : i + 1, :] = rhs_ref[i : i + 1, :] - row_of(tot[4 * i : 4 * i + 4, :])

        @pl.when(is_q)
        def _():
            acc[0:1, :] = res_ref[0:1, :]

    def x_copy(j, o):
        return rcopy(xs.at[j], xs.at[j], s_xss.at[o], s_xsr.at[j], ((j + o) % 8, 0))

    def x_recv(j):
        rcopy(xs.at[j], xs.at[j], s_xss.at[0], s_xsr.at[j], ((p + 1) % 8, 0)).wait_recv()

    def ev_c(j):
        @pl.when(is_q & (p > j))
        def _():
            blk = a_v.at[pl.ds(0, B)] if j == 0 else chb.at[j - 1]
            if j:
                rcopy(a_v.at[pl.ds(0, B)], chb.at[j - 1], s_blks, s_blkr.at[j - 1], ((p + 1) % 8, 0)).wait_recv()
            x_recv(j)
            row = row_of(xs[j, 0:4, :]).astype(bf16)
            acc[0:1, :] = acc[0:1, :] - dot_t(jnp.broadcast_to(row, (16, B)), blk[...])[0:1, :]

        @pl.when(is_q & (p == j))
        def _():
            if j == 0:
                pass
            s = acc[0:1, :]
            hi = s.astype(bf16).astype(f32)
            mid = (s - hi).astype(bf16).astype(f32)
            lo = (s - hi - mid).astype(bf16).astype(f32)
            k = lax.broadcasted_iota(jnp.int32, (16, B), 0)
            lhs = jnp.where(k == 0, hi, jnp.where(k == 1, mid, jnp.where(k == 2, lo, 0.0)))
            r3 = dot_t(lhs.astype(bf16), inv_v[...])
            x = (r3[0:1, :] + r3[1:2, :]) + r3[2:3, :]
            for m in range(4):
                xs[j, m : m + 1, :] = x[:, 128 * m : 128 * (m + 1)]
            xs[j, 4:8, :] = jnp.zeros((4, 128), f32)
            for o in (1, 2, 3, 4, 5, 6, 7):
                x_copy(j, o).start()

    def fz_copy(o):
        return rcopy(xs, xs, s_fs.at[o], s_fz, (p, zm[o]))

    def fy_copy(o):
        return rcopy(xs, xs, s_fs.at[7 + o], s_fy, (p, ym[o]))

    def ev_f0():
        @pl.when(is_q)
        def _():
            for j in range(8):
                pl.when(p < j)(lambda j=j: x_recv(j))
            for o in (3, 4, 2, 5, 1, 6, 0):
                fz_copy(o).start()
            for o in range(3):
                fy_copy(o).start()

    def ev_f1():
        @pl.when((y == 0) & (z != 0))
        def _():
            fz_copy(0).wait_recv()
            for o in range(3):
                fy_copy(o).start()

    def ev_f2():
        pl.when(y != 0)(lambda: fy_copy(0).wait_recv())
        for j in range(8):
            pre_ref[j : j + 1, :] = row_of(xs[j, 0:4, :])

    def tri(m, low):
        a = lax.broadcasted_iota(jnp.int32, (B, B), 0)
        b = lax.broadcasted_iota(jnp.int32, (B, B), 1)
        return jnp.where((a >= b) if low else (a <= b), m.astype(f32), 0.0).astype(bf16)

    def ev_v():
        ld_u.wait()
        ld_l.wait()
        for k in range(2):
            u_v[k] = tri(u_v[k], False)
            l_v[k] = tri(l_v[k], True)

    def ev_x():
        @pl.when(p >= 2)
        def _():
            rcopy(xb.at[core], xb.at[core], s_xsend.at[0], s_prim, (p, nbr[0])).wait_recv()
            xb_pair().start()

        rcopy(xb.at[1 - core], xb.at[1 - core], s_xsend.at[0], s_oth, (p, nbr[0])).wait_recv()
        v_f[...] = dot(u_v[0], dot(l_v[0], xb[0]).astype(bf16))

    def c_copy(r):
        mine = comf.at[r, pl.ds(pl.multiple_of(256 * core, 256), 256)]
        return rcopy(strm.at[r, pl.ds(4 * B, 256)], mine, s_cs.at[r], s_cr.at[r], (p + 1 - 2 * core, q))

    def ev_com():
        for r in range(2):
            c_copy(r).start()
            comf[r, pl.ds(pl.multiple_of(256 * core, 256), 256)] = strm[r, 4 * B : 4 * B + 256]

    def ev_w():
        for r in range(2):
            other = comf.at[r, pl.ds(pl.multiple_of(256 - 256 * core, 256), 256)]
            rcopy(other, other, s_cs.at[r], s_cr.at[r], (p + 1 - 2 * core, q)).wait_recv()
        v = v_f[...]
        d = (xb[1].astype(f32) - dot(comf[0], v.astype(bf16))).astype(bf16)
        w1 = dot(u_v[1], dot(l_v[1], d).astype(bf16)).astype(bf16)
        w_v[1] = w1
        v1 = dot(u_v[0], dot(l_v[0], comf[1]).astype(bf16)).astype(bf16)
        w_v[0] = (v - dot(v1, w1)).astype(bf16)

    last = NC - 1 + lag(MAXD) + 1
    com_tick = NPOS + NCC + lag(MAXD)
    events = [
        (0, ev_v), (1, ev_y), (2, ev_z),
        (NPOS, lambda: com_ready()),
    ]
    for j in range(8):
        events.append((min(2 + j, last), lambda j=j: ev_c(j)))
    events += [(9, ev_x), (10, ev_f0), (12, ev_f1), (com_tick, ev_com), (com_tick + 1, ev_w)]

    def com_ready():
        for r in range(2):
            pl.when((q == r) & jnp.logical_not(src_com))(lambda r=r: com_copy(0).wait_recv())
        inject(NPOS, NC)

    ld_i.wait()
    now = 0
    for when, ev in sorted(events, key=lambda e: e[0]):
        when = min(when, last)
        if when > now:
            ticks(now, when)
            now = when
        ev()
    if now < last:
        ticks(now, last)

    def step(s, c):
        i256 = pl.ds(pl.multiple_of(s * 256, 256), 256)
        prod = dot(strm[0, i256], w_v[0]) + dot(strm[1, i256], w_v[1])
        out_v[i256] = (a_v[i256].astype(f32) - prod).astype(bf16)
        pltpu.make_async_copy(out_v.at[i256], out_hbm.at[i256], s_out).start()
        return c

    lax.fori_loop(0, 8, step, 0)
    ev_f2()

    for r, t, lg, kids in info:
        for d in range(4):
            sent = strm.at[r, pl.ds(0, NC * CH)]
            pl.when(kids[d] == 1)(
                lambda r=r, t=t, d=d, sent=sent: rcopy(sent, sent, s_send.at[r, t, d], s_recv.at[r, t, 0], (p, nbr[d])).wait_send()
            )
    for o in range(3):
        ry_copy(o).wait_send()
    for o in range(7):
        rz_copy(o).wait_send()

    @pl.when(src_com)
    def _():
        for o in range(7):
            com_copy(o).wait_send()

    for j in range(1, 7):
        pl.when((q == j) & (p > j))(lambda j=j: blk_copy(j).wait_send())
    xb_pair().wait_send()

    @pl.when(p < 2)
    def _():
        for o in range(3):
            xb_copy(o).wait_send()

    for r in range(2):
        c_copy(r).wait_send()

    @pl.when(is_q)
    def _():
        for o in range(1, 8):
            x_copy(0, o).wait_send()
        for o in range(7):
            fz_copy(o).wait_send()

    @pl.when(y == 0)
    def _():
        for o in range(3):
            fy_copy(o).wait_send()

    pltpu.make_async_copy(out_v, out_hbm, s_out).wait()


def shards(matrix, upper_inv, lower_inv, solution, right_side, diagonal_block_inverses):
    dma, vm = pltpu.SemaphoreType.DMA, pltpu.VMEM
    hbm = pl.BlockSpec(memory_space=pl.ANY)
    vmem = pl.BlockSpec(memory_space=pltpu.VMEM)
    updated, residual, precond = pl.pallas_call(
        kernel,
        out_shape=(
            jax.ShapeDtypeStruct((4 * B, B), bf16),
            jax.ShapeDtypeStruct((4, B), f32),
            jax.ShapeDtypeStruct((8, B), f32),
        ),
        in_specs=[hbm, hbm, hbm, vmem, vmem, hbm],
        out_specs=(hbm, vmem, vmem),
        scratch_shapes=[
            vm((4 * B, B), bf16), vm((2, 4 * B + 256, B), bf16), vm((2, B, B), bf16), vm((2, B, B), bf16),
            vm((B, B), bf16), vm((6, B, B), bf16), vm((2, B, B), bf16), vm((2, B, B), bf16), vm((2, B, B), bf16),
            vm((B, B), f32), vm((4, 16, 128), f32), vm((8, 16, 128), f32), vm((8, 8, 128), f32), vm((8, B), f32),
            vm((4 * B, B), bf16),
            dma((7,)), dma, dma((2, 4, 4)), dma((2, 4, NC)), dma((4,)), dma, dma, dma((7,)), dma,
            dma, dma((6,)), dma((3,)), dma((4,)), dma((7,)), dma((8,)), dma((8,)), dma((8,)), dma((10,)), dma, dma,
            dma((2,)), dma((2,)),
        ],
        compiler_params=pltpu.CompilerParams(collective_id=0, has_side_effects=True, vmem_limit_bytes=56 << 20),
        cost_estimate=pl.CostEstimate(flops=8 << 30, bytes_accessed=8 << 20, transcendentals=0),
    )(
        matrix.reshape(4 * B, B),
        upper_inv,
        lower_inv,
        solution.reshape(1, B),
        right_side.reshape(4, B),
        diagonal_block_inverses.reshape(B, B),
    )
    return updated.reshape(matrix.shape), residual.reshape(right_side.shape), precond


def solution(mesh):
    return jax.shard_map(
        shards,
        mesh=mesh,
        in_specs=(
            P(None, "prow", None, None, "pcol", None),
            P(),
            P(),
            P(None, "pcol", None),
            P(None, "prow", None),
            P(None, "prow", None, None),
        ),
        out_specs=(P(None, "prow", None, None, "pcol", None), P(None, "prow", None), P()),
        check_vma=False,
    )
```

```python
import jax
import jax.numpy as jnp
from jax import lax
from jax.experimental import pallas as pl
from jax.experimental.pallas import tpu as pltpu
from jax.sharding import PartitionSpec as P

MESH = pl.DeviceIdType.MESH
B = 512
CH = 64
CR = 16
NPOS = 3
NC = B // CH + 1
DIRS = ((1, 0), (-1, 0), (0, 1), (0, -1))
TABLE = (
    (
        (2049, 221261, 184641, 147824, 27936, 217255, 151904, 95728, 53056, 69879, 246113, 115112, 85856, 229655, 145761, 101824, 109488, 141619, 190849, 141760, 125360, 198994, 254353, 158160, 182576, 229643, 205177, 254356, 237984, 229563, 194432, 254432),
        (1032, 237952, 66900, 64752, 164736, 254416, 205191, 117664, 188728, 156096, 138720, 126928, 196872, 229736, 181696, 131864, 237786, 246056, 173400, 140042, 213163, 229657, 152932, 120768, 147563, 155828, 126448, 112544, 82506, 106788, 221364, 70310),
    ),
    (
        (205006, 2050, 147856, 201010, 151799, 11104, 62448, 152016, 78087, 44896, 156056, 196962, 254247, 69424, 93040, 129330, 158019, 85376, 133552, 190834, 207185, 141808, 158160, 229730, 213259, 158016, 197012, 229722, 221435, 172368, 246192, 210768),
        (123360, 520, 23360, 74660, 205248, 124352, 60896, 229815, 147952, 139528, 85984, 121792, 246120, 155880, 99624, 140224, 205128, 213177, 140553, 181048, 254218, 180395, 128848, 168772, 180388, 163947, 71552, 117728, 164068, 82969, 62613, 196916),
    ),
)
ROOT_DIR = ((0, 2, 3, 1), (1, 2, 3, 0))
LAG_MAX = 31
EY = 2
EZ = 7
EX = 15
EC = (8, 10, 13, 16, 19, 21, 24, 27)
EF0 = 30
EF1 = 33
EP = 99
EW = 99
f32, bf16 = jnp.float32, jnp.bfloat16


def dot(a, b):
    return jnp.dot(a, b, preferred_element_type=f32)


def dot_t(a, b):
    return lax.dot_general(a, b, (((1,), (1,)), ((), ())), preferred_element_type=f32)


def row_of(c):
    return jnp.concatenate([c[m : m + 1, :] for m in range(4)], axis=1)


def kernel(
    a_hbm, u_hbm, l_hbm, sol_ref, rhs_ref, inv_hbm,
    out_hbm, res_ref, pre_ref,
    a_v, strm, u_v, l_v, inv_v, chb, xb, comf, w_v, v_f, ry, rz, xs, pk, acc, out_v,
    s_loc, s_out, s_send, s_recv, s_xsend, s_prim, s_oth, s_comsend, s_comx,
    s_blks, s_blkr, s_rys, s_ryr, s_rzs, s_rzr, s_xss, s_xsr, s_fs, s_fz, s_fy, s_cs, s_cr, s_gs, s_gr,
):
    p = lax.axis_index("prow")
    q = lax.axis_index("pcol")
    core = p % 2
    y, z = q % 4, q // 4
    is_q = q == 0

    def at(dy, dz):
        return ((z + dz + 8) % 8) * 4 + (y + dy + 4) % 4

    def rcopy(src, dst, ss, rs, dev):
        return pltpu.make_async_remote_copy(
            src_ref=src, dst_ref=dst, send_sem=ss, recv_sem=rs, device_id=dev, device_id_type=MESH
        )

    ld_a = pltpu.make_async_copy(a_hbm, a_v, s_loc.at[0])
    ld_u = pltpu.make_async_copy(u_hbm, u_v, s_loc.at[1])
    ld_l = pltpu.make_async_copy(l_hbm, l_v, s_loc.at[2])
    ld_i = pltpu.make_async_copy(inv_hbm, inv_v, s_loc.at[3])
    ld_a.start()
    for r in range(2):
        pl.when(q == r)(lambda r=r: pltpu.make_async_copy(a_hbm, strm.at[r, pl.ds(0, 4 * B)], s_loc.at[4]).start())
    src_com = (p + q) == 1

    def piece(d):
        return pl.ds(pl.multiple_of(64 * (4 * (d % 2) + d // 2), 64), 64)

    def com_own():
        return pltpu.make_async_copy(
            a_hbm.at[piece(p)], strm.at[q, pl.ds(4 * B, 64)], s_loc.at[5]
        )

    pl.when(src_com)(lambda: com_own().start())

    def xb_own():
        return pltpu.make_async_copy(a_hbm.at[pl.ds(0, B)], xb.at[core], s_loc.at[6])

    pl.when(p < 2)(lambda: xb_own().start())
    ld_u.start()
    ld_l.start()
    ld_i.start()

    def tri(m, low):
        a = lax.broadcasted_iota(jnp.int32, (B, B), 0)
        b = lax.broadcasted_iota(jnp.int32, (B, B), 1)
        return jnp.where((a >= b) if low else (a <= b), m.astype(f32), 0.0).astype(bf16)

    def ev_v():
        ld_u.wait()
        ld_l.wait()
        for k in range(2):
            u_v[k] = tri(u_v[k], False)
            l_v[k] = tri(l_v[k], True)

    bar = pltpu.get_barrier_semaphore()
    zm = [at(0, o) for o in range(1, 8)]
    ym = [at(o, 0) for o in range(1, 4)]
    pm = [(p + o) % 8 for o in range(1, 8)]
    for o in (3, 4, 2, 5, 1, 6, 0):
        pl.semaphore_signal(bar, inc=1, device_id=(p, zm[o]), device_id_type=MESH)
    for d in pm:
        pl.semaphore_signal(bar, inc=1, device_id=(d, q), device_id_type=MESH)
    for d in ym:
        pl.semaphore_signal(bar, inc=1, device_id=(p, d), device_id_type=MESH)

    @pl.when((q == 5) | (q == 6))
    def _():
        pl.semaphore_signal(bar, inc=1, device_id=(p, 0), device_id_type=MESH)

    @pl.when(is_q)
    def _():
        for d in (5, 6):
            pl.semaphore_signal(bar, inc=1, device_id=(p, d), device_id_type=MESH)

    ld_a.wait()
    sol8 = jnp.broadcast_to(sol_ref[...], (16, B))
    for i in range(4):
        part = dot_t(sol8, a_v[i * B : (i + 1) * B, :])
        for m in range(4):
            ry[y, 4 * i + m : 4 * i + m + 1, :] = part[0:1, 128 * m : 128 * (m + 1)]
    info = []
    for r in range(2):
        for h in range(2):
            word = jnp.int32(0)
            for k in range(32):
                word = jnp.where(q == k, jnp.int32(TABLE[r][h][k]), word)
            for t in range(2):
                v = (word // (512**t)) % 512
                mask = v % 16
                info.append((r, 2 * h + t, v // 16, [(mask // (1 << d)) % 2 for d in range(4)]))
    nbr = [at(dy, dz) for dy, dz in DIRS]
    for r in range(2):
        pl.when(q == r)(lambda r=r: pltpu.make_async_copy(a_hbm, strm.at[r, pl.ds(0, 4 * B)], s_loc.at[4]).wait())
    ev_v()
    ld_i.wait()
    pl.semaphore_wait(bar, 17 + jnp.where(is_q, 2, jnp.where((q == 5) | (q == 6), 1, 0)))

    def hop(r, t, n, d):
        part = strm.at[r, pl.ds(pl.multiple_of(B * t + CH * jnp.where(n > NPOS, n - 1, n), CH), CH)]
        return rcopy(part, part, s_send.at[r, t, d], s_recv.at[r, t, n], (p, nbr[d]))

    def com_hop(r, t, d):
        part = strm.at[r, pl.ds(4 * B + CR * t, CR)]
        return rcopy(part, part, s_send.at[r, t, d], s_recv.at[r, t, NPOS], (p, nbr[d]))

    def inject(lo, hi):
        for r in range(2):

            @pl.when(q == r)
            def _():
                def one(n, c):
                    for t in range(4):
                        hop(r, t, n, ROOT_DIR[r][t]).start()
                    return c

                lax.fori_loop(lo, hi, one, 0)

    def ry_copy(o):
        return rcopy(ry.at[y], ry.at[y], s_rys.at[o], s_ryr.at[y], (p, ym[o]))

    for o in range(3):
        ry_copy(o).start()
    inject(0, NPOS)

    def com_copy(o):
        return rcopy(
            a_v.at[piece(pm[o])], strm.at[q, pl.ds(4 * B, 64)], s_comsend.at[o], s_comx, (pm[o], q)
        )

    @pl.when(src_com)
    def _():
        for o in (0, 1, 6, 5, 2, 4, 3):
            com_copy(o).start()
        com_own().wait()

    def blk_copy(j):
        return rcopy(a_v.at[pl.ds(0, B)], chb.at[j - 1], s_blks, s_blkr.at[j - 1], (p, 0))

    for j in range(1, 7):
        pl.when((q == j) & (p > j))(lambda j=j: blk_copy(j).start())

    def xb_copy(o):
        return rcopy(xb.at[core], xb.at[core], s_xsend.at[o], s_prim, (2 * (o + 1) + core, q))

    def xb_pair():
        return rcopy(xb.at[core], xb.at[core], s_xsend.at[3], s_oth, (p + 1 - 2 * core, q))

    @pl.when(p < 2)
    def _():
        xb_own().wait()
        xb_pair().start()
        for o in (0, 2, 1):
            xb_copy(o).start()

    def ticks(lo, hi):
        def one(k, c):
            for r, t, lg, kids in info:
                n = k - lg
                other = q != r

                @pl.when((n >= 0) & (n < NC) & (n != NPOS) & other)
                def _():
                    hop(r, t, n, 0).wait_recv()
                    for d in range(4):
                        pl.when(kids[d] == 1)(lambda d=d: hop(r, t, n, d).start())

                @pl.when((n == NPOS) & other)
                def _():
                    com_hop(r, t, 0).wait_recv()
                    for d in range(4):
                        pl.when(kids[d] == 1)(lambda d=d: com_hop(r, t, d).start())

            return c

        lax.fori_loop(lo, hi, one, 0)

    def rz_copy(o):
        return rcopy(rz.at[z], rz.at[z], s_rzs.at[o], s_rzr.at[z], (p, zm[o]))

    def ev_y():
        for o in range(1, 4):
            src = (y + o) % 4
            rcopy(ry.at[src], ry.at[src], s_rys.at[0], s_ryr.at[src], (p, ym[0])).wait_recv()
        rz[z] = ((ry[0] + ry[1]) + (ry[2] + ry[3]))
        for o in (3, 4, 2, 5, 1, 6, 0):
            rz_copy(o).start()

    def ev_z():
        for o in range(1, 8):
            src = (z + o) % 8
            rcopy(rz.at[src], rz.at[src], s_rzs.at[0], s_rzr.at[src], (p, zm[0])).wait_recv()
        tot = rz[0]
        for k in range(1, 8):
            tot = tot + rz[k]
        for i in range(4):
            res_ref[i] = rhs_ref[i] - row_of(tot[4 * i : 4 * i + 4, :])

        @pl.when(is_q)
        def _():
            acc[0:1, :] = res_ref[0]

    def x_copy(j, o):
        return rcopy(xs.at[j], xs.at[j], s_xss.at[o], s_xsr.at[j], ((j + o) % 8, 0))

    def x_recv(j):
        rcopy(xs.at[j], xs.at[j], s_xss.at[0], s_xsr.at[j], ((p + 1) % 8, 0)).wait_recv()

    def ev_c(j):
        @pl.when(is_q & (p > j))
        def _():
            blk = a_v.at[pl.ds(0, B)] if j == 0 else chb.at[j - 1]
            if j:
                rcopy(a_v.at[pl.ds(0, B)], chb.at[j - 1], s_blks, s_blkr.at[j - 1], ((p + 1) % 8, 0)).wait_recv()
            x_recv(j)
            row = row_of(xs[j, 0:4, :]).astype(bf16)
            acc[0:1, :] = acc[0:1, :] - dot_t(jnp.broadcast_to(row, (16, B)), blk[...])[0:1, :]

        @pl.when(is_q & (p == j))
        def _():
            if j == 0:
                pass
            s = acc[0:1, :]
            hi = s.astype(bf16).astype(f32)
            mid = (s - hi).astype(bf16).astype(f32)
            lo = (s - hi - mid).astype(bf16).astype(f32)
            k = lax.broadcasted_iota(jnp.int32, (16, B), 0)
            lhs = jnp.where(k == 0, hi, jnp.where(k == 1, mid, jnp.where(k == 2, lo, 0.0)))
            r3 = dot_t(lhs.astype(bf16), inv_v[...])
            x = (r3[0:1, :] + r3[1:2, :]) + r3[2:3, :]
            for m in range(4):
                xs[j, m : m + 1, :] = x[:, 128 * m : 128 * (m + 1)]
            xs[j, 4:8, :] = jnp.zeros((4, 128), f32)
            for o in (1, 2, 3, 4, 5, 6, 7):
                x_copy(j, o).start()

    def fz_copy(o):
        return rcopy(pk, pk, s_fs.at[o], s_fz, (p, zm[o]))

    def fy_copy(o):
        return rcopy(pk, pk, s_fs.at[7 + o], s_fy, (p, ym[o]))

    def ev_f0():
        @pl.when(is_q)
        def _():
            for j in range(8):
                pl.when(p < j)(lambda j=j: x_recv(j))
            for j in range(8):
                pk[4 * j : 4 * j + 4, :] = xs[j, 0:4, :]
            for o in (3, 4, 2, 5, 1, 6, 0):
                fz_copy(o).start()
            for o in range(3):
                fy_copy(o).start()

    def ev_f1():
        @pl.when((y == 0) & (z != 0))
        def _():
            fz_copy(0).wait_recv()
            for o in range(3):
                fy_copy(o).start()

    def ev_f2():
        pl.when(y != 0)(lambda: fy_copy(0).wait_recv())
        for j in range(8):
            pre_ref[j : j + 1, :] = row_of(pk[4 * j : 4 * j + 4, :])

    def ev_x():
        @pl.when(p >= 2)
        def _():
            rcopy(xb.at[core], xb.at[core], s_xsend.at[0], s_prim, (p, nbr[0])).wait_recv()
            xb_pair().start()

        rcopy(xb.at[1 - core], xb.at[1 - core], s_xsend.at[0], s_oth, (p, nbr[0])).wait_recv()
        v_f[...] = dot(u_v[0], dot(l_v[0], xb[0]).astype(bf16))

    half = pl.ds(pl.multiple_of(256 * core, 256), 256)

    def g_copy(r, o):
        return rcopy(
            strm.at[r, pl.ds(4 * B, 64)], comf.at[r, piece(p)], s_gs.at[r, o], s_gr.at[r, p // 2], (pm[2 * o + 1], q)
        )

    def c_copy(r):
        return rcopy(comf.at[r, half], comf.at[r, half], s_cs.at[r], s_cr.at[r], (p + 1 - 2 * core, q))

    def ev_com():
        for r in range(2):
            for o in range(3):
                g_copy(r, o).start()
            comf[r, piece(p)] = strm[r, 4 * B : 4 * B + 64]

    def ev_pair():
        for r in range(2):
            for o in range(3):
                src = pm[2 * o + 1]
                rcopy(
                    strm.at[r, pl.ds(4 * B, 64)], comf.at[r, piece(src)], s_gs.at[r, o], s_gr.at[r, src // 2], (src, q)
                ).wait_recv()
            c_copy(r).start()

    def ev_w():
        for r in range(2):
            other = comf.at[r, pl.ds(pl.multiple_of(256 - 256 * core, 256), 256)]
            rcopy(other, other, s_cs.at[r], s_cr.at[r], (p + 1 - 2 * core, q)).wait_recv()
        v = v_f[...]
        d = (xb[1].astype(f32) - dot(comf[0], v.astype(bf16))).astype(bf16)
        w1 = dot(u_v[1], dot(l_v[1], d).astype(bf16)).astype(bf16)
        w_v[1] = w1
        v1 = dot(u_v[0], dot(l_v[0], comf[1]).astype(bf16)).astype(bf16)
        w_v[0] = (v - dot(v1, w1)).astype(bf16)

    last = NC + LAG_MAX
    events = [(0, lambda: com_ready()), (EY, ev_y), (EZ, ev_z), (EX, ev_x), (EF0, ev_f0), (EF1, ev_f1)]
    events += [(EC[j], lambda j=j: ev_c(j)) for j in range(8)]
    events += [(NPOS + 1 + LAG_MAX, ev_com), (EP, ev_pair), (EW, ev_w)]

    def com_ready():
        for r in range(2):
            pl.when((q == r) & jnp.logical_not(src_com))(lambda r=r: com_copy(0).wait_recv())
        for r in range(2):
            pl.when(q == r)(lambda r=r: [com_hop(r, t, ROOT_DIR[r][t]).start() for t in range(4)] and None)
        inject(NPOS + 1, NC)

    now = 0
    for when, ev in sorted(events, key=lambda e: e[0]):
        when = min(when, last)
        if when > now:
            ticks(now, when)
            now = when
        ev()
    if now < last:
        ticks(now, last)

    def step(s, c):
        i256 = pl.ds(pl.multiple_of(s * 256, 256), 256)
        prod = dot(strm[0, i256], w_v[0]) + dot(strm[1, i256], w_v[1])
        out_v[i256] = (a_v[i256].astype(f32) - prod).astype(bf16)
        pltpu.make_async_copy(out_v.at[i256], out_hbm.at[i256], s_out).start()
        return c

    lax.fori_loop(0, 8, step, 0)
    ev_f2()

    for r, t, lg, kids in info:
        for d in range(4):
            sent = strm.at[r, pl.ds(0, B + CR)]
            pl.when(kids[d] == 1)(
                lambda r=r, t=t, d=d, sent=sent: rcopy(sent, sent, s_send.at[r, t, d], s_recv.at[r, t, 0], (p, nbr[d])).wait_send()
            )
    for o in range(3):
        ry_copy(o).wait_send()
    for o in range(7):
        rz_copy(o).wait_send()

    @pl.when(src_com)
    def _():
        for o in range(7):
            com_copy(o).wait_send()

    for j in range(1, 7):
        pl.when((q == j) & (p > j))(lambda j=j: blk_copy(j).wait_send())
    xb_pair().wait_send()

    @pl.when(p < 2)
    def _():
        for o in range(3):
            xb_copy(o).wait_send()

    for r in range(2):
        c_copy(r).wait_send()
        for o in range(3):
            g_copy(r, o).wait_send()

    @pl.when(is_q)
    def _():
        for o in range(1, 8):
            x_copy(0, o).wait_send()
        for o in range(7):
            fz_copy(o).wait_send()

    @pl.when(y == 0)
    def _():
        for o in range(3):
            fy_copy(o).wait_send()

    pltpu.make_async_copy(out_v, out_hbm, s_out).wait()


def shards(matrix, upper_inv, lower_inv, solution, right_side, diagonal_block_inverses):
    dma, vm = pltpu.SemaphoreType.DMA, pltpu.VMEM
    hbm = pl.BlockSpec(memory_space=pl.ANY)
    vmem = pl.BlockSpec(memory_space=pltpu.VMEM)
    updated, residual, precond = pl.pallas_call(
        kernel,
        out_shape=(
            jax.ShapeDtypeStruct((4 * B, B), bf16),
            jax.ShapeDtypeStruct((4, 1, B), f32),
            jax.ShapeDtypeStruct((8, B), f32),
        ),
        in_specs=[hbm, hbm, hbm, vmem, vmem, hbm],
        out_specs=(hbm, vmem, vmem),
        scratch_shapes=[
            vm((4 * B, B), bf16), vm((2, 4 * B + 64, B), bf16), vm((2, B, B), bf16), vm((2, B, B), bf16),
            vm((B, B), bf16), vm((6, B, B), bf16), vm((2, B, B), bf16), vm((2, B, B), bf16), vm((2, B, B), bf16),
            vm((B, B), f32), vm((4, 16, 128), f32), vm((8, 16, 128), f32), vm((8, 8, 128), f32), vm((32, 128), f32), vm((8, B), f32),
            vm((4 * B, B), bf16),
            dma((7,)), dma, dma((2, 4, 4)), dma((2, 4, NC)), dma((4,)), dma, dma, dma((7,)), dma,
            dma, dma((6,)), dma((3,)), dma((4,)), dma((7,)), dma((8,)), dma((8,)), dma((8,)), dma((10,)), dma, dma,
            dma((2,)), dma((2,)), dma((2, 3)), dma((2, 4)),
        ],
        compiler_params=pltpu.CompilerParams(collective_id=0, has_side_effects=True, vmem_limit_bytes=56 << 20),
        cost_estimate=pl.CostEstimate(flops=8 << 30, bytes_accessed=8 << 20, transcendentals=0),
    )(
        matrix.reshape(4 * B, B),
        upper_inv,
        lower_inv,
        solution.reshape(1, B),
        right_side,
        diagonal_block_inverses.reshape(B, B),
    )
    return updated.reshape(matrix.shape), residual, precond


def solution(mesh):
    return jax.shard_map(
        shards,
        mesh=mesh,
        in_specs=(
            P(None, "prow", None, None, "pcol", None),
            P(),
            P(),
            P(None, "pcol", None),
            P(None, "prow", None),
            P(None, "prow", None, None),
        ),
        out_specs=(P(None, "prow", None, None, "pcol", None), P(None, "prow", None), P()),
        check_vma=False,
    )
```

```python
import jax
import jax.numpy as jnp
from jax import lax
from jax.experimental import pallas as pl
from jax.experimental.pallas import tpu as pltpu
from jax.sharding import PartitionSpec as P

MESH = pl.DeviceIdType.MESH
B = 512
CH = 64
CR = 16
ND = B // CH
DIRS = ((1, 0), (-1, 0), (0, 1), (0, -1))
TABLE = (
    (
        (65537, 183240781, 148513089, 122168688, 34446624, 174723751, 122299232, 78557680, 52027712, 60954871, 200811361, 104343976, 78242656, 191896855, 122102625, 87141824, 95775664, 121970483, 157099905, 121974208, 104672176, 165749586, 209463697, 130887120, 148447024, 191896331, 174335353, 209463700, 192162208, 191894203, 157214592, 209465312),
        (32776, 192161664, 69247828, 60791024, 139487104, 209464784, 174335879, 104425888, 157032248, 130821568, 121876448, 113110480, 165681928, 191898472, 148417984, 121658648, 192157402, 200810280, 148153176, 121920266, 174592683, 191896857, 122332004, 104525248, 122162283, 130814644, 104706544, 95873440, 78137418, 95690020, 183243956, 69358246),
    ),
    (
        (174331086, 65538, 122169744, 165814066, 122296567, 17130336, 60715504, 122301904, 69606151, 43377504, 130820504, 165684066, 209460519, 60940080, 78472560, 104800050, 130883907, 78227328, 113322928, 157099378, 174400337, 121975280, 130887120, 191898978, 182983435, 130883904, 165685652, 191898458, 183245051, 148120400, 200813488, 174515024),
        (104607712, 16392, 25911616, 69495204, 174337472, 104639936, 60665824, 191900599, 122171888, 121903880, 78245856, 104558016, 200811368, 130816232, 87072040, 121925056, 174334280, 174593209, 121936649, 148397880, 209459978, 148378283, 104784720, 139616580, 148378276, 139463787, 69396352, 104427488, 139466980, 78152729, 60723349, 165682996),
    ),
)
ROOT_DIR = ((0, 2, 3, 1), (1, 2, 3, 0))
NPOS = 3
EY = 2
EZ = 7
EX = 13
EC = 8
ECS = 3
EF0 = 31
EF1 = 34
PD = 9
PW = 2
LAST = 39
f32, bf16 = jnp.float32, jnp.bfloat16


def dot(a, b):
    return jnp.dot(a, b, preferred_element_type=f32)


def dot_t(a, b):
    return lax.dot_general(a, b, (((1,), (1,)), ((), ())), preferred_element_type=f32)


def row_of(c):
    return jnp.concatenate([c[m : m + 1, :] for m in range(4)], axis=1)


def kernel(
    a_hbm, u_hbm, l_hbm, sol_ref, rhs_ref, inv_hbm,
    out_hbm, res_ref, pre_ref,
    a_v, strm, u_v, l_v, inv_v, chb, xb, comf, w_v, v_f, ry, rz, xs, pk, acc, out_v,
    s_loc, s_out, s_send, s_recv, s_xsend, s_prim, s_oth, s_comsend, s_comx,
    s_blks, s_blkr, s_rys, s_ryr, s_rzs, s_rzr, s_xss, s_xsr, s_fs, s_fz, s_fy, s_cs, s_cr, s_gs, s_gr,
):
    p = lax.axis_index("prow")
    q = lax.axis_index("pcol")
    core = p % 2
    y, z = q % 4, q // 4
    is_q = q == 0

    def at(dy, dz):
        return ((z + dz + 8) % 8) * 4 + (y + dy + 4) % 4

    def rcopy(src, dst, ss, rs, dev):
        return pltpu.make_async_remote_copy(
            src_ref=src, dst_ref=dst, send_sem=ss, recv_sem=rs, device_id=dev, device_id_type=MESH
        )

    ld_a = pltpu.make_async_copy(a_hbm, a_v, s_loc.at[0])
    ld_u = pltpu.make_async_copy(u_hbm, u_v, s_loc.at[1])
    ld_l = pltpu.make_async_copy(l_hbm, l_v, s_loc.at[2])
    ld_i = pltpu.make_async_copy(inv_hbm, inv_v, s_loc.at[3])
    ld_a.start()
    for r in range(2):
        pl.when(q == r)(lambda r=r: pltpu.make_async_copy(a_hbm, strm.at[r, pl.ds(0, 4 * B)], s_loc.at[4]).start())
    src_com = (p + q) == 1

    def piece(d):
        return pl.ds(pl.multiple_of(64 * (4 * (d % 2) + d // 2), 64), 64)

    def com_own():
        return pltpu.make_async_copy(
            a_hbm.at[piece(p)], strm.at[q, pl.ds(4 * B, 64)], s_loc.at[5]
        )

    pl.when(src_com)(lambda: com_own().start())

    def xb_own():
        return pltpu.make_async_copy(a_hbm.at[pl.ds(0, B)], xb.at[core], s_loc.at[6])

    pl.when(p < 2)(lambda: xb_own().start())
    ld_u.start()
    ld_l.start()
    ld_i.start()

    def tri(m, low):
        a = lax.broadcasted_iota(jnp.int32, (B, B), 0)
        b = lax.broadcasted_iota(jnp.int32, (B, B), 1)
        return jnp.where((a >= b) if low else (a <= b), m.astype(f32), 0.0).astype(bf16)

    def ev_v():
        ld_u.wait()
        ld_l.wait()
        for k in range(2):
            u_v[k] = tri(u_v[k], False)
            l_v[k] = tri(l_v[k], True)

    bar = pltpu.get_barrier_semaphore()
    zm = [at(0, o) for o in range(1, 8)]
    ym = [at(o, 0) for o in range(1, 4)]
    pm = [(p + o) % 8 for o in range(1, 8)]
    for o in (3, 4, 2, 5, 1, 6, 0):
        pl.semaphore_signal(bar, inc=1, device_id=(p, zm[o]), device_id_type=MESH)
    for d in pm:
        pl.semaphore_signal(bar, inc=1, device_id=(d, q), device_id_type=MESH)
    for d in ym:
        pl.semaphore_signal(bar, inc=1, device_id=(p, d), device_id_type=MESH)

    @pl.when((q == 5) | (q == 6))
    def _():
        pl.semaphore_signal(bar, inc=1, device_id=(p, 0), device_id_type=MESH)

    @pl.when(is_q)
    def _():
        for d in (5, 6):
            pl.semaphore_signal(bar, inc=1, device_id=(p, d), device_id_type=MESH)

    ld_a.wait()
    sol8 = jnp.broadcast_to(sol_ref[...], (16, B))
    for i in range(4):
        part = dot_t(sol8, a_v[i * B : (i + 1) * B, :])
        for m in range(4):
            ry[y, 4 * i + m : 4 * i + m + 1, :] = part[0:1, 128 * m : 128 * (m + 1)]
    info = []
    for r in range(2):
        for h in range(2):
            word = jnp.int32(0)
            for k in range(32):
                word = jnp.where(q == k, jnp.int32(TABLE[r][h][k]), word)
            for t in range(2):
                v = (word // (16384**t)) % 16384
                kids = [(v // (1 << d)) % 2 for d in range(4)]
                info.append((r, 2 * h + t, (v // 16) % 32, v // 512, kids))
    com_tick = jnp.int32(0)
    for r, t, lg, clg, kids in info:
        com_tick = jnp.maximum(com_tick, clg + 1)
    w_tick = jnp.maximum(com_tick + PD + PW, EX + 1)
    nbr = [at(dy, dz) for dy, dz in DIRS]
    for r in range(2):
        pl.when(q == r)(lambda r=r: pltpu.make_async_copy(a_hbm, strm.at[r, pl.ds(0, 4 * B)], s_loc.at[4]).wait())
    ev_v()
    ld_i.wait()
    pl.semaphore_wait(bar, 17 + jnp.where(is_q, 2, jnp.where((q == 5) | (q == 6), 1, 0)))

    def hop(r, t, n, d):
        part = strm.at[r, pl.ds(pl.multiple_of(B * t + CH * n, CH), CH)]
        return rcopy(part, part, s_send.at[r, t, d], s_recv.at[r, t, n], (p, nbr[d]))

    def com_hop(r, t, d):
        part = strm.at[r, pl.ds(4 * B + CR * t, CR)]
        return rcopy(part, part, s_send.at[r, t, d], s_recv.at[r, t, ND], (p, nbr[d]))

    def inject(lo, hi):
        for r in range(2):

            @pl.when(q == r)
            def _():
                def one(n, c):
                    for t in range(4):
                        hop(r, t, n, ROOT_DIR[r][t]).start()
                    return c

                lax.fori_loop(lo, hi, one, 0)

    def ry_copy(o):
        return rcopy(ry.at[y], ry.at[y], s_rys.at[o], s_ryr.at[y], (p, ym[o]))

    for o in range(3):
        ry_copy(o).start()
    inject(0, NPOS)

    def com_copy(o):
        return rcopy(
            a_v.at[piece(pm[o])], strm.at[q, pl.ds(4 * B, 64)], s_comsend.at[o], s_comx, (pm[o], q)
        )

    @pl.when(src_com)
    def _():
        for o in (0, 1, 6, 5, 2, 4, 3):
            com_copy(o).start()
        com_own().wait()

    def blk_copy(j):
        return rcopy(a_v.at[pl.ds(0, B)], chb.at[j], s_blks, s_blkr.at[j], (p, 0))

    for j in range(1, 7):
        pl.when((q == j) & (p > j))(lambda j=j: blk_copy(j).start())
    pl.when(is_q & (p > 0))(lambda: pltpu.make_async_copy(a_hbm.at[pl.ds(0, B)], chb.at[0], s_blkr.at[0]).start())

    def xb_copy(o):
        return rcopy(xb.at[core], xb.at[core], s_xsend.at[o], s_prim, (2 * (o + 1) + core, q))

    def xb_pair():
        return rcopy(xb.at[core], xb.at[core], s_xsend.at[3], s_oth, (p + 1 - 2 * core, q))

    @pl.when(p < 2)
    def _():
        xb_own().wait()
        xb_pair().start()
        for o in (0, 2, 1):
            xb_copy(o).start()

    def streams(k):
        for r, t, lg, clg, kids in info:
            n = k - lg
            other = q != r

            @pl.when((n >= 0) & (n < ND) & other)
            def _():
                hop(r, t, n, 0).wait_recv()
                for d in range(4):
                    pl.when(kids[d] == 1)(lambda d=d: hop(r, t, n, d).start())

            @pl.when((k == clg) & other)
            def _():
                com_hop(r, t, 0).wait_recv()
                for d in range(4):
                    pl.when(kids[d] == 1)(lambda d=d: com_hop(r, t, d).start())

    def rz_copy(o):
        return rcopy(rz.at[z], rz.at[z], s_rzs.at[o], s_rzr.at[z], (p, zm[o]))

    def ev_y():
        for o in range(1, 4):
            src = (y + o) % 4
            rcopy(ry.at[src], ry.at[src], s_rys.at[0], s_ryr.at[src], (p, ym[0])).wait_recv()
        rz[z] = ((ry[0] + ry[1]) + (ry[2] + ry[3]))
        for o in (3, 4, 2, 5, 1, 6, 0):
            rz_copy(o).start()

    def ev_z():
        for o in range(1, 8):
            src = (z + o) % 8
            rcopy(rz.at[src], rz.at[src], s_rzs.at[0], s_rzr.at[src], (p, zm[0])).wait_recv()
        tot = rz[0]
        for k in range(1, 8):
            tot = tot + rz[k]
        for i in range(4):
            res_ref[i] = rhs_ref[i] - row_of(tot[4 * i : 4 * i + 4, :])

        @pl.when(is_q)
        def _():
            acc[0:1, :] = res_ref[0]

    def x_copy(j, o):
        return rcopy(xs.at[j], xs.at[j], s_xss.at[o], s_xsr.at[j], ((j + o) % 8, 0))

    def x_recv(j):
        rcopy(xs.at[j], xs.at[j], s_xss.at[0], s_xsr.at[j], ((p + 1) % 8, 0)).wait_recv()

    def ev_c(j):
        @pl.when(is_q & (p > j))
        def _():
            rcopy(a_v.at[pl.ds(0, B)], chb.at[j], s_blks, s_blkr.at[j], ((p + 1) % 8, 0)).wait_recv()
            x_recv(j)
            row = row_of(xs[j, 0:4, :]).astype(bf16)
            acc[0:1, :] = acc[0:1, :] - dot_t(jnp.broadcast_to(row, (16, B)), chb[j])[0:1, :]

        @pl.when(is_q & (p == j))
        def _():
            s = acc[0:1, :]
            hi = s.astype(bf16).astype(f32)
            mid = (s - hi).astype(bf16).astype(f32)
            lo = (s - hi - mid).astype(bf16).astype(f32)
            k = lax.broadcasted_iota(jnp.int32, (16, B), 0)
            lhs = jnp.where(k == 0, hi, jnp.where(k == 1, mid, jnp.where(k == 2, lo, 0.0)))
            r3 = dot_t(lhs.astype(bf16), inv_v[...])
            x = (r3[0:1, :] + r3[1:2, :]) + r3[2:3, :]
            for m in range(4):
                xs[j, m : m + 1, :] = x[:, 128 * m : 128 * (m + 1)]
            xs[j, 4:8, :] = jnp.zeros((4, 128), f32)
            for o in (1, 2, 3, 4, 5, 6, 7):
                x_copy(j, o).start()

    def fz_copy(o):
        return rcopy(pk, pk, s_fs.at[o], s_fz, (p, zm[o]))

    def fy_copy(o):
        return rcopy(pk, pk, s_fs.at[7 + o], s_fy, (p, ym[o]))

    def ev_f0():
        @pl.when(is_q)
        def _():
            for j in range(8):
                pl.when(p < j)(lambda j=j: x_recv(j))
            for j in range(8):
                pk[4 * j : 4 * j + 4, :] = xs[j, 0:4, :]
            for o in (3, 4, 2, 5, 1, 6, 0):
                fz_copy(o).start()
            for o in range(3):
                fy_copy(o).start()

    def ev_f1():
        @pl.when((y == 0) & (z != 0))
        def _():
            fz_copy(0).wait_recv()
            for o in range(3):
                fy_copy(o).start()

    def ev_f2():
        pl.when(y != 0)(lambda: fy_copy(0).wait_recv())
        for j in range(8):
            pre_ref[j : j + 1, :] = row_of(pk[4 * j : 4 * j + 4, :])

    def ev_x():
        @pl.when(p >= 2)
        def _():
            rcopy(xb.at[core], xb.at[core], s_xsend.at[0], s_prim, (p, nbr[0])).wait_recv()
            xb_pair().start()

        rcopy(xb.at[1 - core], xb.at[1 - core], s_xsend.at[0], s_oth, (p, nbr[0])).wait_recv()
        v_f[...] = dot(u_v[0], dot(l_v[0], xb[0]).astype(bf16))

    half = pl.ds(pl.multiple_of(256 * core, 256), 256)

    def g_copy(r, o):
        return rcopy(
            strm.at[r, pl.ds(4 * B, 64)], comf.at[r, piece(p)], s_gs.at[r, o], s_gr.at[r, p // 2], (pm[2 * o + 1], q)
        )

    def c_copy(r):
        return rcopy(comf.at[r, half], comf.at[r, half], s_cs.at[r], s_cr.at[r], (p + 1 - 2 * core, q))

    def ev_com():
        for r in range(2):
            for o in range(3):
                g_copy(r, o).start()
            comf[r, piece(p)] = strm[r, 4 * B : 4 * B + 64]

    def ev_pair():
        for r in range(2):
            for o in range(3):
                src = pm[2 * o + 1]
                rcopy(
                    strm.at[r, pl.ds(4 * B, 64)], comf.at[r, piece(src)], s_gs.at[r, o], s_gr.at[r, src // 2], (src, q)
                ).wait_recv()
            c_copy(r).start()

    def ev_w():
        for r in range(2):
            other = comf.at[r, pl.ds(pl.multiple_of(256 - 256 * core, 256), 256)]
            rcopy(other, other, s_cs.at[r], s_cr.at[r], (p + 1 - 2 * core, q)).wait_recv()
        v = v_f[...]
        d = (xb[1].astype(f32) - dot(comf[0], v.astype(bf16))).astype(bf16)
        w1 = dot(u_v[1], dot(l_v[1], d).astype(bf16)).astype(bf16)
        w_v[1] = w1
        v1 = dot(u_v[0], dot(l_v[0], comf[1]).astype(bf16)).astype(bf16)
        w_v[0] = (v - dot(v1, w1)).astype(bf16)

    def com_ready():
        for r in range(2):
            pl.when((q == r) & jnp.logical_not(src_com))(lambda r=r: com_copy(0).wait_recv())
        for r in range(2):
            pl.when(q == r)(lambda r=r: [com_hop(r, t, ROOT_DIR[r][t]).start() for t in range(4)] and None)
        inject(NPOS, ND)

    com_ready()
    events = ((EY, ev_y), (EZ, ev_z), (EX, ev_x), (EF0, ev_f0), (EF1, ev_f1))

    def tick(k, c):
        for when, ev in events:
            pl.when(k == when)(ev)
        pl.when((k >= EC) & ((k - EC) % ECS == 0) & (k < EC + 8 * ECS))(lambda: ev_c((k - EC) // ECS))
        pl.when(k == com_tick)(ev_com)
        pl.when(k == com_tick + PD)(ev_pair)
        pl.when(k == w_tick)(ev_w)
        streams(k)
        return c

    lax.fori_loop(0, LAST, tick, 0)

    def step(s, c):
        i256 = pl.ds(pl.multiple_of(s * 256, 256), 256)
        prod = dot(strm[0, i256], w_v[0]) + dot(strm[1, i256], w_v[1])
        out_v[i256] = (a_v[i256].astype(f32) - prod).astype(bf16)
        pltpu.make_async_copy(out_v.at[i256], out_hbm.at[i256], s_out).start()
        return c

    lax.fori_loop(0, 8, step, 0)
    ev_f2()

    for r, t, lg, clg, kids in info:
        for d in range(4):
            sent = strm.at[r, pl.ds(0, B + CR)]
            pl.when(kids[d] == 1)(
                lambda r=r, t=t, d=d, sent=sent: rcopy(sent, sent, s_send.at[r, t, d], s_recv.at[r, t, 0], (p, nbr[d])).wait_send()
            )
    for o in range(3):
        ry_copy(o).wait_send()
    for o in range(7):
        rz_copy(o).wait_send()

    @pl.when(src_com)
    def _():
        for o in range(7):
            com_copy(o).wait_send()

    for j in range(1, 7):
        pl.when((q == j) & (p > j))(lambda j=j: blk_copy(j).wait_send())
    xb_pair().wait_send()

    @pl.when(p < 2)
    def _():
        for o in range(3):
            xb_copy(o).wait_send()

    for r in range(2):
        c_copy(r).wait_send()
        for o in range(3):
            g_copy(r, o).wait_send()

    @pl.when(is_q)
    def _():
        for o in range(1, 8):
            x_copy(0, o).wait_send()
        for o in range(7):
            fz_copy(o).wait_send()

    @pl.when(y == 0)
    def _():
        for o in range(3):
            fy_copy(o).wait_send()

    pltpu.make_async_copy(out_v, out_hbm, s_out).wait()


def shards(matrix, upper_inv, lower_inv, solution, right_side, diagonal_block_inverses):
    dma, vm = pltpu.SemaphoreType.DMA, pltpu.VMEM
    hbm = pl.BlockSpec(memory_space=pl.ANY)
    vmem = pl.BlockSpec(memory_space=pltpu.VMEM)
    updated, residual, precond = pl.pallas_call(
        kernel,
        out_shape=(
            jax.ShapeDtypeStruct((4 * B, B), bf16),
            jax.ShapeDtypeStruct((4, 1, B), f32),
            jax.ShapeDtypeStruct((8, B), f32),
        ),
        in_specs=[hbm, hbm, hbm, vmem, vmem, hbm],
        out_specs=(hbm, vmem, vmem),
        scratch_shapes=[
            vm((4 * B, B), bf16), vm((2, 4 * B + 64, B), bf16), vm((2, B, B), bf16), vm((2, B, B), bf16),
            vm((B, B), bf16), vm((7, B, B), bf16), vm((2, B, B), bf16), vm((2, B, B), bf16), vm((2, B, B), bf16),
            vm((B, B), f32), vm((4, 16, 128), f32), vm((8, 16, 128), f32), vm((8, 8, 128), f32), vm((32, 128), f32), vm((8, B), f32),
            vm((4 * B, B), bf16),
            dma((7,)), dma, dma((2, 4, 4)), dma((2, 4, ND + 1)), dma((4,)), dma, dma, dma((7,)), dma,
            dma, dma((7,)), dma((3,)), dma((4,)), dma((7,)), dma((8,)), dma((8,)), dma((8,)), dma((10,)), dma, dma,
            dma((2,)), dma((2,)), dma((2, 3)), dma((2, 4)),
        ],
        compiler_params=pltpu.CompilerParams(collective_id=0, has_side_effects=True, vmem_limit_bytes=56 << 20),
        cost_estimate=pl.CostEstimate(flops=8 << 30, bytes_accessed=8 << 20, transcendentals=0),
    )(
        matrix.reshape(4 * B, B),
        upper_inv,
        lower_inv,
        solution.reshape(1, B),
        right_side,
        diagonal_block_inverses.reshape(B, B),
    )
    return updated.reshape(matrix.shape), residual, precond


def solution(mesh):
    return jax.shard_map(
        shards,
        mesh=mesh,
        in_specs=(
            P(None, "prow", None, None, "pcol", None),
            P(),
            P(),
            P(None, "pcol", None),
            P(None, "prow", None),
            P(None, "prow", None, None),
        ),
        out_specs=(P(None, "prow", None, None, "pcol", None), P(None, "prow", None), P()),
        check_vma=False,
    )
```

```python
import jax
import jax.numpy as jnp
from jax import lax
from jax.experimental import pallas as pl
from jax.experimental.pallas import tpu as pltpu
from jax.sharding import PartitionSpec as P

MESH = pl.DeviceIdType.MESH
B = 512
CH = 64
CR = 16
ND = B // CH
DIRS = ((1, 0), (-1, 0), (0, 1), (0, -1))
TABLE = (
    (
        (65537, 183240781, 148513089, 122168688, 34446624, 174723751, 122299232, 78557680, 52027712, 60954871, 200811361, 104343976, 78242656, 191896855, 122102625, 87141824, 95775664, 121970483, 157099905, 121974208, 104672176, 165749586, 209463697, 130887120, 148447024, 191896331, 174335353, 209463700, 192162208, 191894203, 157214592, 209465312),
        (32776, 192161664, 69247828, 60791024, 139487104, 209464784, 174335879, 104425888, 157032248, 130821568, 121876448, 113110480, 165681928, 191898472, 148417984, 121658648, 192157402, 200810280, 148153176, 121920266, 174592683, 191896857, 122332004, 104525248, 122162283, 130814644, 104706544, 95873440, 78137418, 95690020, 183243956, 69358246),
    ),
    (
        (174331086, 65538, 122169744, 165814066, 122296567, 17130336, 60715504, 122301904, 69606151, 43377504, 130820504, 165684066, 209460519, 60940080, 78472560, 104800050, 130883907, 78227328, 113322928, 157099378, 174400337, 121975280, 130887120, 191898978, 182983435, 130883904, 165685652, 191898458, 183245051, 148120400, 200813488, 174515024),
        (104607712, 16392, 25911616, 69495204, 174337472, 104639936, 60665824, 191900599, 122171888, 121903880, 78245856, 104558016, 200811368, 130816232, 87072040, 121925056, 174334280, 174593209, 121936649, 148397880, 209459978, 148378283, 104784720, 139616580, 148378276, 139463787, 69396352, 104427488, 139466980, 78152729, 60723349, 165682996),
    ),
)
ROOT_DIR = ((0, 2, 3, 1), (1, 2, 3, 0))
NPOS = 3
EY = 2
EZ = 7
EX = 11
EC = 8
ECS = 3
EF0 = 31
EF1 = 34
PD = 10
PW = 2
LAST = 39
f32, bf16 = jnp.float32, jnp.bfloat16


def dot(a, b):
    return jnp.dot(a, b, preferred_element_type=f32)


def dot_t(a, b):
    return lax.dot_general(a, b, (((1,), (1,)), ((), ())), preferred_element_type=f32)


def row_of(c):
    return jnp.concatenate([c[m : m + 1, :] for m in range(4)], axis=1)


def kernel(
    a_hbm, u_hbm, l_hbm, sol_ref, rhs_ref, inv_hbm,
    out_hbm, res_ref, pre_ref,
    a_v, strm, u_v, l_v, inv_v, chb, xb, comf, w_v, v_f, ry, rz, xs, pk, acc, out_v,
    s_loc, s_out, s_send, s_recv, s_xsend, s_prim, s_oth, s_comsend, s_comx,
    s_blks, s_blkr, s_rys, s_ryr, s_rzs, s_rzr, s_xss, s_xsr, s_fs, s_fz, s_fy, s_cs, s_cr, s_gs, s_gr,
):
    p = lax.axis_index("prow")
    q = lax.axis_index("pcol")
    core = p % 2
    y, z = q % 4, q // 4
    is_q = q == 0

    def at(dy, dz):
        return ((z + dz + 8) % 8) * 4 + (y + dy + 4) % 4

    def rcopy(src, dst, ss, rs, dev):
        return pltpu.make_async_remote_copy(
            src_ref=src, dst_ref=dst, send_sem=ss, recv_sem=rs, device_id=dev, device_id_type=MESH
        )

    ld_a = pltpu.make_async_copy(a_hbm, a_v, s_loc.at[0])
    ld_u = pltpu.make_async_copy(u_hbm, u_v, s_loc.at[1])
    ld_l = pltpu.make_async_copy(l_hbm, l_v, s_loc.at[2])
    ld_i = pltpu.make_async_copy(inv_hbm, inv_v, s_loc.at[3])
    ld_a.start()
    for r in range(2):
        pl.when(q == r)(lambda r=r: pltpu.make_async_copy(a_hbm, strm.at[r, pl.ds(0, 4 * B)], s_loc.at[4]).start())
    src_com = (p + q) == 1

    def piece(d):
        return pl.ds(pl.multiple_of(64 * (4 * (d % 2) + d // 2), 64), 64)

    def com_own():
        return pltpu.make_async_copy(
            a_hbm.at[piece(p)], strm.at[q, pl.ds(4 * B, 64)], s_loc.at[5]
        )

    pl.when(src_com)(lambda: com_own().start())

    def xb_own():
        return pltpu.make_async_copy(a_hbm.at[pl.ds(0, B)], xb.at[core], s_loc.at[6])

    pl.when(p < 2)(lambda: xb_own().start())
    ld_u.start()
    ld_l.start()
    ld_i.start()

    def tri(m, low):
        a = lax.broadcasted_iota(jnp.int32, (B, B), 0)
        b = lax.broadcasted_iota(jnp.int32, (B, B), 1)
        return jnp.where((a >= b) if low else (a <= b), m.astype(f32), 0.0).astype(bf16)

    def ev_v():
        ld_u.wait()
        ld_l.wait()
        for k in range(2):
            u_v[k] = tri(u_v[k], False)
            l_v[k] = tri(l_v[k], True)

    bar = pltpu.get_barrier_semaphore()
    zm = [at(0, o) for o in range(1, 8)]
    ym = [at(o, 0) for o in range(1, 4)]
    pm = [(p + o) % 8 for o in range(1, 8)]
    for o in (3, 4, 2, 5, 1, 6, 0):
        pl.semaphore_signal(bar, inc=1, device_id=(p, zm[o]), device_id_type=MESH)
    for d in pm:
        pl.semaphore_signal(bar, inc=1, device_id=(d, q), device_id_type=MESH)
    for d in ym:
        pl.semaphore_signal(bar, inc=1, device_id=(p, d), device_id_type=MESH)

    @pl.when((q == 5) | (q == 6))
    def _():
        pl.semaphore_signal(bar, inc=1, device_id=(p, 0), device_id_type=MESH)

    @pl.when(is_q)
    def _():
        for d in (5, 6):
            pl.semaphore_signal(bar, inc=1, device_id=(p, d), device_id_type=MESH)

    ld_a.wait()
    sol8 = jnp.broadcast_to(sol_ref[...], (16, B))
    for i in range(4):
        part = dot_t(sol8, a_v[i * B : (i + 1) * B, :])
        for m in range(4):
            ry[y, 4 * i + m : 4 * i + m + 1, :] = part[0:1, 128 * m : 128 * (m + 1)]
    info = []
    for r in range(2):
        for h in range(2):
            word = jnp.int32(0)
            for k in range(32):
                word = jnp.where(q == k, jnp.int32(TABLE[r][h][k]), word)
            for t in range(2):
                v = (word // (16384**t)) % 16384
                kids = [(v // (1 << d)) % 2 for d in range(4)]
                info.append((r, 2 * h + t, (v // 16) % 32, v // 512, kids))
    com_tick = jnp.int32(0)
    for r, t, lg, clg, kids in info:
        com_tick = jnp.maximum(com_tick, clg + 1)
    w_tick = jnp.maximum(com_tick + PD + PW, EX + 1)
    nbr = [at(dy, dz) for dy, dz in DIRS]
    for r in range(2):
        pl.when(q == r)(lambda r=r: pltpu.make_async_copy(a_hbm, strm.at[r, pl.ds(0, 4 * B)], s_loc.at[4]).wait())
    ev_v()
    ld_i.wait()
    pl.semaphore_wait(bar, 17 + jnp.where(is_q, 2, jnp.where((q == 5) | (q == 6), 1, 0)))

    def hop(r, t, n, d):
        part = strm.at[r, pl.ds(pl.multiple_of(B * t + CH * n, CH), CH)]
        return rcopy(part, part, s_send.at[r, t, d], s_recv.at[r, t, n], (p, nbr[d]))

    def com_hop(r, t, d):
        part = strm.at[r, pl.ds(4 * B + CR * t, CR)]
        return rcopy(part, part, s_send.at[r, t, d], s_recv.at[r, t, ND], (p, nbr[d]))

    def inject(lo, hi):
        for r in range(2):

            @pl.when(q == r)
            def _():
                def one(n, c):
                    for t in range(4):
                        hop(r, t, n, ROOT_DIR[r][t]).start()
                    return c

                lax.fori_loop(lo, hi, one, 0)

    def ry_copy(o):
        return rcopy(ry.at[y], ry.at[y], s_rys.at[o], s_ryr.at[y], (p, ym[o]))

    for o in range(3):
        ry_copy(o).start()
    inject(0, NPOS)

    def com_copy(o):
        return rcopy(
            a_v.at[piece(pm[o])], strm.at[q, pl.ds(4 * B, 64)], s_comsend.at[o], s_comx, (pm[o], q)
        )

    @pl.when(src_com)
    def _():
        for o in (0, 1, 6, 5, 2, 4, 3):
            com_copy(o).start()
        com_own().wait()

    def blk_copy(j):
        return rcopy(a_v.at[pl.ds(0, B)], chb.at[j], s_blks, s_blkr.at[j], (p, 0))

    for j in range(1, 7):
        pl.when((q == j) & (p > j))(lambda j=j: blk_copy(j).start())
    pl.when(is_q & (p > 0))(lambda: pltpu.make_async_copy(a_hbm.at[pl.ds(0, B)], chb.at[0], s_blkr.at[0]).start())

    def xb_copy(o):
        return rcopy(xb.at[core], xb.at[core], s_xsend.at[o], s_prim, (2 * (o + 1) + core, q))

    def xb_pair():
        return rcopy(xb.at[core], xb.at[core], s_xsend.at[3], s_oth, (p + 1 - 2 * core, q))

    @pl.when(p < 2)
    def _():
        xb_own().wait()
        xb_pair().start()
        for o in (0, 2, 1):
            xb_copy(o).start()

    def streams(k):
        for r, t, lg, clg, kids in info:
            n = k - lg
            other = q != r

            @pl.when((n >= 0) & (n < ND) & other)
            def _():
                hop(r, t, n, 0).wait_recv()
                for d in range(4):
                    pl.when(kids[d] == 1)(lambda d=d: hop(r, t, n, d).start())

            @pl.when((k == clg) & other)
            def _():
                com_hop(r, t, 0).wait_recv()
                for d in range(4):
                    pl.when(kids[d] == 1)(lambda d=d: com_hop(r, t, d).start())

    def rz_copy(o):
        return rcopy(rz.at[z], rz.at[z], s_rzs.at[o], s_rzr.at[z], (p, zm[o]))

    def ev_y():
        for o in range(1, 4):
            src = (y + o) % 4
            rcopy(ry.at[src], ry.at[src], s_rys.at[0], s_ryr.at[src], (p, ym[0])).wait_recv()
        rz[z] = ((ry[0] + ry[1]) + (ry[2] + ry[3]))
        for o in (3, 4, 2, 5, 1, 6, 0):
            rz_copy(o).start()

    def ev_z():
        for o in range(1, 8):
            src = (z + o) % 8
            rcopy(rz.at[src], rz.at[src], s_rzs.at[0], s_rzr.at[src], (p, zm[0])).wait_recv()
        tot = rz[0]
        for k in range(1, 8):
            tot = tot + rz[k]
        for i in range(4):
            res_ref[i] = rhs_ref[i] - row_of(tot[4 * i : 4 * i + 4, :])

        @pl.when(is_q)
        def _():
            acc[0:1, :] = res_ref[0]

    def x_copy(j, o):
        return rcopy(xs.at[j], xs.at[j], s_xss.at[o], s_xsr.at[j], ((j + o) % 8, 0))

    def x_recv(j):
        rcopy(xs.at[j], xs.at[j], s_xss.at[0], s_xsr.at[j], ((p + 1) % 8, 0)).wait_recv()

    def ev_c(j):
        @pl.when(is_q & (p > j))
        def _():
            rcopy(a_v.at[pl.ds(0, B)], chb.at[j], s_blks, s_blkr.at[j], ((p + 1) % 8, 0)).wait_recv()
            x_recv(j)
            row = row_of(xs[j, 0:4, :]).astype(bf16)
            acc[0:1, :] = acc[0:1, :] - dot_t(jnp.broadcast_to(row, (16, B)), chb[j])[0:1, :]

        @pl.when(is_q & (p == j))
        def _():
            s = acc[0:1, :]
            hi = s.astype(bf16).astype(f32)
            mid = (s - hi).astype(bf16).astype(f32)
            lo = (s - hi - mid).astype(bf16).astype(f32)
            k = lax.broadcasted_iota(jnp.int32, (16, B), 0)
            lhs = jnp.where(k == 0, hi, jnp.where(k == 1, mid, jnp.where(k == 2, lo, 0.0)))
            r3 = dot_t(lhs.astype(bf16), inv_v[...])
            x = (r3[0:1, :] + r3[1:2, :]) + r3[2:3, :]
            for m in range(4):
                xs[j, m : m + 1, :] = x[:, 128 * m : 128 * (m + 1)]
            xs[j, 4:8, :] = jnp.zeros((4, 128), f32)
            for o in (1, 2, 3, 4, 5, 6, 7):
                x_copy(j, o).start()

    def fz_copy(o):
        return rcopy(pk, pk, s_fs.at[o], s_fz, (p, zm[o]))

    def fy_copy(o):
        return rcopy(pk, pk, s_fs.at[7 + o], s_fy, (p, ym[o]))

    def ev_f0():
        @pl.when(is_q)
        def _():
            for j in range(8):
                pl.when(p < j)(lambda j=j: x_recv(j))
            for j in range(8):
                pk[4 * j : 4 * j + 4, :] = xs[j, 0:4, :]
            for o in (3, 4, 2, 5, 1, 6, 0):
                fz_copy(o).start()
            for o in range(3):
                fy_copy(o).start()

    def ev_f1():
        @pl.when((y == 0) & (z != 0))
        def _():
            fz_copy(0).wait_recv()
            for o in range(3):
                fy_copy(o).start()

    def ev_f2():
        pl.when(y != 0)(lambda: fy_copy(0).wait_recv())
        for j in range(8):
            pre_ref[j : j + 1, :] = row_of(pk[4 * j : 4 * j + 4, :])

    def ev_x():
        @pl.when(p >= 2)
        def _():
            rcopy(xb.at[core], xb.at[core], s_xsend.at[0], s_prim, (p, nbr[0])).wait_recv()
            xb_pair().start()

        rcopy(xb.at[1 - core], xb.at[1 - core], s_xsend.at[0], s_oth, (p, nbr[0])).wait_recv()
        v_f[...] = dot(u_v[0], dot(l_v[0], xb[0]).astype(bf16))

    half = pl.ds(pl.multiple_of(256 * core, 256), 256)

    def g_copy(r, o):
        return rcopy(
            strm.at[r, pl.ds(4 * B, 64)], comf.at[r, piece(p)], s_gs.at[r, o], s_gr.at[r, p // 2], (pm[2 * o + 1], q)
        )

    def c_copy(r):
        return rcopy(comf.at[r, half], comf.at[r, half], s_cs.at[r], s_cr.at[r], (p + 1 - 2 * core, q))

    def ev_com():
        for r in range(2):
            for o in range(3):
                g_copy(r, o).start()
            comf[r, piece(p)] = strm[r, 4 * B : 4 * B + 64]

    def ev_pair():
        for r in range(2):
            for o in range(3):
                src = pm[2 * o + 1]
                rcopy(
                    strm.at[r, pl.ds(4 * B, 64)], comf.at[r, piece(src)], s_gs.at[r, o], s_gr.at[r, src // 2], (src, q)
                ).wait_recv()
            c_copy(r).start()

    def ev_w():
        for r in range(2):
            other = comf.at[r, pl.ds(pl.multiple_of(256 - 256 * core, 256), 256)]
            rcopy(other, other, s_cs.at[r], s_cr.at[r], (p + 1 - 2 * core, q)).wait_recv()
        v = v_f[...]
        d = (xb[1].astype(f32) - dot(comf[0], v.astype(bf16))).astype(bf16)
        w1 = dot(u_v[1], dot(l_v[1], d).astype(bf16)).astype(bf16)
        w_v[1] = w1
        v1 = dot(u_v[0], dot(l_v[0], comf[1]).astype(bf16)).astype(bf16)
        w_v[0] = (v - dot(v1, w1)).astype(bf16)

    def com_ready():
        for r in range(2):
            pl.when((q == r) & jnp.logical_not(src_com))(lambda r=r: com_copy(0).wait_recv())
        for r in range(2):
            pl.when(q == r)(lambda r=r: [com_hop(r, t, ROOT_DIR[r][t]).start() for t in range(4)] and None)
        inject(NPOS, ND)

    com_ready()
    events = ((EY, ev_y), (EZ, ev_z), (EX, ev_x), (EF0, ev_f0), (EF1, ev_f1))

    def tick(k, c):
        for when, ev in events:
            pl.when(k == when)(ev)
        pl.when((k >= EC) & ((k - EC) % ECS == 0) & (k < EC + 8 * ECS))(lambda: ev_c((k - EC) // ECS))
        pl.when(k == com_tick)(ev_com)
        pl.when(k == com_tick + PD)(ev_pair)
        pl.when(k == w_tick)(ev_w)
        streams(k)
        return c

    lax.fori_loop(0, LAST, tick, 0)

    def step(s, c):
        i256 = pl.ds(pl.multiple_of(s * 256, 256), 256)
        prod = dot(strm[0, i256], w_v[0]) + dot(strm[1, i256], w_v[1])
        out_v[i256] = (a_v[i256].astype(f32) - prod).astype(bf16)
        pltpu.make_async_copy(out_v.at[i256], out_hbm.at[i256], s_out).start()
        return c

    lax.fori_loop(0, 8, step, 0)
    ev_f2()

    for r, t, lg, clg, kids in info:
        for d in range(4):
            sent = strm.at[r, pl.ds(0, B + CR)]
            pl.when(kids[d] == 1)(
                lambda r=r, t=t, d=d, sent=sent: rcopy(sent, sent, s_send.at[r, t, d], s_recv.at[r, t, 0], (p, nbr[d])).wait_send()
            )
    for o in range(3):
        ry_copy(o).wait_send()
    for o in range(7):
        rz_copy(o).wait_send()

    @pl.when(src_com)
    def _():
        for o in range(7):
            com_copy(o).wait_send()

    for j in range(1, 7):
        pl.when((q == j) & (p > j))(lambda j=j: blk_copy(j).wait_send())
    xb_pair().wait_send()

    @pl.when(p < 2)
    def _():
        for o in range(3):
            xb_copy(o).wait_send()

    for r in range(2):
        c_copy(r).wait_send()
        for o in range(3):
            g_copy(r, o).wait_send()

    @pl.when(is_q)
    def _():
        for o in range(1, 8):
            x_copy(0, o).wait_send()
        for o in range(7):
            fz_copy(o).wait_send()

    @pl.when(y == 0)
    def _():
        for o in range(3):
            fy_copy(o).wait_send()

    pltpu.make_async_copy(out_v, out_hbm, s_out).wait()


def hand_out(a_hbm, res_in, pre_in, out_hbm, res_out, pre_out, buf, res_v, pre_v, s_in, s_out):
    steps = [(a_hbm.at[w], buf.at[w], out_hbm.at[w]) for w in (pl.ds(256 * k, 256) for k in range(8))]
    steps = [(res_in, res_v, res_out), (pre_in, pre_v, pre_out)] + steps
    ins = [pltpu.make_async_copy(a, b, s_in.at[k]) for k, (a, b, c) in enumerate(steps)]
    outs = [pltpu.make_async_copy(b, c, s_out.at[k]) for k, (a, b, c) in enumerate(steps)]
    for c in ins:
        c.start()
    for c, o in zip(ins, outs):
        c.wait()
        o.start()
    for o in outs:
        o.wait()


def shards(matrix, upper_inv, lower_inv, solution, right_side, diagonal_block_inverses):
    dma, vm = pltpu.SemaphoreType.DMA, pltpu.VMEM
    hbm = pl.BlockSpec(memory_space=pl.ANY)
    vmem = pl.BlockSpec(memory_space=pltpu.VMEM)
    updated, residual, precond = pl.pallas_call(
        kernel,
        out_shape=(
            jax.ShapeDtypeStruct((4 * B, B), bf16),
            jax.ShapeDtypeStruct((4, 1, B), f32),
            jax.ShapeDtypeStruct((8, B), f32),
        ),
        in_specs=[hbm, hbm, hbm, vmem, vmem, hbm],
        out_specs=(hbm, vmem, vmem),
        scratch_shapes=[
            vm((4 * B, B), bf16), vm((2, 4 * B + 64, B), bf16), vm((2, B, B), bf16), vm((2, B, B), bf16),
            vm((B, B), bf16), vm((7, B, B), bf16), vm((2, B, B), bf16), vm((2, B, B), bf16), vm((2, B, B), bf16),
            vm((B, B), f32), vm((4, 16, 128), f32), vm((8, 16, 128), f32), vm((8, 8, 128), f32), vm((32, 128), f32), vm((8, B), f32),
            vm((4 * B, B), bf16),
            dma((7,)), dma, dma((2, 4, 4)), dma((2, 4, ND + 1)), dma((4,)), dma, dma, dma((7,)), dma,
            dma, dma((7,)), dma((3,)), dma((4,)), dma((7,)), dma((8,)), dma((8,)), dma((8,)), dma((10,)), dma, dma,
            dma((2,)), dma((2,)), dma((2, 3)), dma((2, 4)),
        ],
        compiler_params=pltpu.CompilerParams(collective_id=0, has_side_effects=True, vmem_limit_bytes=56 << 20),
        cost_estimate=pl.CostEstimate(flops=8 << 30, bytes_accessed=8 << 20, transcendentals=0),
    )(
        matrix.reshape(4 * B, B),
        upper_inv,
        lower_inv,
        solution.reshape(1, B),
        right_side,
        diagonal_block_inverses.reshape(B, B),
    )
    updated, residual, precond = pl.pallas_call(
        hand_out,
        out_shape=(
            jax.ShapeDtypeStruct((4 * B, B), bf16),
            jax.ShapeDtypeStruct((4, 1, B), f32),
            jax.ShapeDtypeStruct((8, B), f32),
        ),
        in_specs=[hbm, hbm, hbm],
        out_specs=(hbm, hbm, hbm),
        scratch_shapes=[vm((4 * B, B), bf16), vm((4, 1, B), f32), vm((8, B), f32), dma((10,)), dma((10,))],
        compiler_params=pltpu.CompilerParams(vmem_limit_bytes=60 << 20),
        cost_estimate=pl.CostEstimate(flops=0, bytes_accessed=4 << 20, transcendentals=0),
    )(updated, residual, precond)
    return updated.reshape(matrix.shape), residual, precond


def solution(mesh):
    return jax.shard_map(
        shards,
        mesh=mesh,
        in_specs=(
            P(None, "prow", None, None, "pcol", None),
            P(),
            P(),
            P(None, "pcol", None),
            P(None, "prow", None),
            P(None, "prow", None, None),
        ),
        out_specs=(P(None, "prow", None, None, "pcol", None), P(None, "prow", None), P()),
        check_vma=False,
    )
```

```python
import jax
import jax.numpy as jnp
from jax import lax
from jax.experimental import pallas as pl
from jax.experimental.pallas import tpu as pltpu
from jax.sharding import PartitionSpec as P

MESH = pl.DeviceIdType.MESH
B = 512
CH = 64
CR = 16
ND = B // CH
DIRS = ((1, 0), (-1, 0), (0, 1), (0, -1))
TABLE = (
    (
        (65537, 183240781, 148513089, 122168688, 34446624, 174723751, 122299232, 78557680, 52027712, 60954871, 200811361, 104343976, 78242656, 191896855, 122102625, 87141824, 95775664, 121970483, 157099905, 121974208, 104672176, 165749586, 209463697, 130887120, 148447024, 191896331, 174335353, 209463700, 192162208, 191894203, 157214592, 209465312),
        (32776, 192161664, 69247828, 60791024, 139487104, 209464784, 174335879, 104425888, 157032248, 130821568, 121876448, 113110480, 165681928, 191898472, 148417984, 121658648, 192157402, 200810280, 148153176, 121920266, 174592683, 191896857, 122332004, 104525248, 122162283, 130814644, 104706544, 95873440, 78137418, 95690020, 183243956, 69358246),
    ),
    (
        (174331086, 65538, 122169744, 165814066, 122296567, 17130336, 60715504, 122301904, 69606151, 43377504, 130820504, 165684066, 209460519, 60940080, 78472560, 104800050, 130883907, 78227328, 113322928, 157099378, 174400337, 121975280, 130887120, 191898978, 182983435, 130883904, 165685652, 191898458, 183245051, 148120400, 200813488, 174515024),
        (104607712, 16392, 25911616, 69495204, 174337472, 104639936, 60665824, 191900599, 122171888, 121903880, 78245856, 104558016, 200811368, 130816232, 87072040, 121925056, 174334280, 174593209, 121936649, 148397880, 209459978, 148378283, 104784720, 139616580, 148378276, 139463787, 69396352, 104427488, 139466980, 78152729, 60723349, 165682996),
    ),
)
ROOT_DIR = ((0, 2, 3, 1), (1, 2, 3, 0))
NPOS = 2
EY = 2
EZ = 7
EX = 11
EC = 8
ECS = 3
EF0 = 31
EF1 = 34
PD = 10
PW = 2
LAST = 39
f32, bf16 = jnp.float32, jnp.bfloat16


def dot(a, b):
    return jnp.dot(a, b, preferred_element_type=f32)


def dot_t(a, b):
    return lax.dot_general(a, b, (((1,), (1,)), ((), ())), preferred_element_type=f32)


def row_of(c):
    return jnp.concatenate([c[m : m + 1, :] for m in range(4)], axis=1)


def kernel(
    a_hbm, u_hbm, l_hbm, sol_ref, rhs_ref, inv_hbm,
    out_hbm, res_ref, pre_ref,
    a_v, strm, u_v, l_v, inv_v, chb, xb, comf, w_v, v_f, ry, rz, xs, pk, acc, out_v,
    s_loc, s_out, s_send, s_recv, s_xsend, s_prim, s_oth, s_comsend, s_comx,
    s_blks, s_blkr, s_rys, s_ryr, s_rzs, s_rzr, s_xss, s_xsr, s_fs, s_fz, s_fy, s_cs, s_cr, s_gs, s_gr,
):
    p = lax.axis_index("prow")
    q = lax.axis_index("pcol")
    core = p % 2
    y, z = q % 4, q // 4
    is_q = q == 0

    def at(dy, dz):
        return ((z + dz + 8) % 8) * 4 + (y + dy + 4) % 4

    def rcopy(src, dst, ss, rs, dev):
        return pltpu.make_async_remote_copy(
            src_ref=src, dst_ref=dst, send_sem=ss, recv_sem=rs, device_id=dev, device_id_type=MESH
        )

    ld_a = pltpu.make_async_copy(a_hbm, a_v, s_loc.at[0])
    ld_u = pltpu.make_async_copy(u_hbm, u_v, s_loc.at[1])
    ld_l = pltpu.make_async_copy(l_hbm, l_v, s_loc.at[2])
    ld_i = pltpu.make_async_copy(inv_hbm, inv_v, s_loc.at[3])
    ld_a.start()
    for r in range(2):
        pl.when(q == r)(lambda r=r: pltpu.make_async_copy(a_hbm, strm.at[r, pl.ds(0, 4 * B)], s_loc.at[4]).start())
    src_com = (p + q) == 1

    def piece(d):
        return pl.ds(pl.multiple_of(64 * (4 * (d % 2) + d // 2), 64), 64)

    def com_own():
        return pltpu.make_async_copy(
            a_hbm.at[piece(p)], strm.at[q, pl.ds(4 * B, 64)], s_loc.at[5]
        )

    pl.when(src_com)(lambda: com_own().start())

    def xb_own():
        return pltpu.make_async_copy(a_hbm.at[pl.ds(0, B)], xb.at[core], s_loc.at[6])

    pl.when(p < 2)(lambda: xb_own().start())
    ld_u.start()
    ld_l.start()
    ld_i.start()

    def tri(m, low):
        a = lax.broadcasted_iota(jnp.int32, (B, B), 0)
        b = lax.broadcasted_iota(jnp.int32, (B, B), 1)
        return jnp.where((a >= b) if low else (a <= b), m.astype(f32), 0.0).astype(bf16)

    def ev_v():
        ld_u.wait()
        ld_l.wait()
        for k in range(2):
            u_v[k] = tri(u_v[k], False)
            l_v[k] = tri(l_v[k], True)

    bar = pltpu.get_barrier_semaphore()
    zm = [at(0, o) for o in range(1, 8)]
    ym = [at(o, 0) for o in range(1, 4)]
    pm = [(p + o) % 8 for o in range(1, 8)]
    for o in (3, 4, 2, 5, 1, 6, 0):
        pl.semaphore_signal(bar, inc=1, device_id=(p, zm[o]), device_id_type=MESH)
    for d in pm:
        pl.semaphore_signal(bar, inc=1, device_id=(d, q), device_id_type=MESH)
    for d in ym:
        pl.semaphore_signal(bar, inc=1, device_id=(p, d), device_id_type=MESH)

    @pl.when((q == 5) | (q == 6))
    def _():
        pl.semaphore_signal(bar, inc=1, device_id=(p, 0), device_id_type=MESH)

    @pl.when(is_q)
    def _():
        for d in (5, 6):
            pl.semaphore_signal(bar, inc=1, device_id=(p, d), device_id_type=MESH)

    ld_a.wait()
    sol8 = jnp.broadcast_to(sol_ref[...], (16, B))
    for i in range(4):
        part = dot_t(sol8, a_v[i * B : (i + 1) * B, :])
        for m in range(4):
            ry[y, 4 * i + m : 4 * i + m + 1, :] = part[0:1, 128 * m : 128 * (m + 1)]
    info = []
    for r in range(2):
        for h in range(2):
            word = jnp.int32(0)
            for k in range(32):
                word = jnp.where(q == k, jnp.int32(TABLE[r][h][k]), word)
            for t in range(2):
                v = (word // (16384**t)) % 16384
                kids = [(v // (1 << d)) % 2 for d in range(4)]
                info.append((r, 2 * h + t, (v // 16) % 32, v // 512, kids))
    com_tick = jnp.int32(0)
    for r, t, lg, clg, kids in info:
        com_tick = jnp.maximum(com_tick, clg + 1)
    w_tick = jnp.maximum(com_tick + PD + PW, EX + 1)
    nbr = [at(dy, dz) for dy, dz in DIRS]
    for r in range(2):
        pl.when(q == r)(lambda r=r: pltpu.make_async_copy(a_hbm, strm.at[r, pl.ds(0, 4 * B)], s_loc.at[4]).wait())
    ev_v()
    ld_i.wait()
    pl.semaphore_wait(bar, 17 + jnp.where(is_q, 2, jnp.where((q == 5) | (q == 6), 1, 0)))

    def hop(r, t, n, d):
        part = strm.at[r, pl.ds(pl.multiple_of(B * t + CH * n, CH), CH)]
        return rcopy(part, part, s_send.at[r, t, d], s_recv.at[r, t, n], (p, nbr[d]))

    def com_hop(r, t, d):
        part = strm.at[r, pl.ds(4 * B + CR * t, CR)]
        return rcopy(part, part, s_send.at[r, t, d], s_recv.at[r, t, ND], (p, nbr[d]))

    def inject(lo, hi):
        for r in range(2):

            @pl.when(q == r)
            def _():
                def one(n, c):
                    for t in range(4):
                        hop(r, t, n, ROOT_DIR[r][t]).start()
                    return c

                lax.fori_loop(lo, hi, one, 0)

    def ry_copy(o):
        return rcopy(ry.at[y], ry.at[y], s_rys.at[o], s_ryr.at[y], (p, ym[o]))

    for o in range(3):
        ry_copy(o).start()
    inject(0, NPOS)

    def com_copy(o):
        return rcopy(
            a_v.at[piece(pm[o])], strm.at[q, pl.ds(4 * B, 64)], s_comsend.at[o], s_comx, (pm[o], q)
        )

    @pl.when(src_com)
    def _():
        for o in (0, 1, 6, 5, 2, 4, 3):
            com_copy(o).start()
        com_own().wait()

    def blk_copy(j):
        return rcopy(a_v.at[pl.ds(0, B)], chb.at[j], s_blks, s_blkr.at[j], (p, 0))

    for j in range(1, 7):
        pl.when((q == j) & (p > j))(lambda j=j: blk_copy(j).start())
    pl.when(is_q & (p > 0))(lambda: pltpu.make_async_copy(a_hbm.at[pl.ds(0, B)], chb.at[0], s_blkr.at[0]).start())

    def xb_copy(o):
        return rcopy(xb.at[core], xb.at[core], s_xsend.at[o], s_prim, (2 * (o + 1) + core, q))

    def xb_pair():
        return rcopy(xb.at[core], xb.at[core], s_xsend.at[3], s_oth, (p + 1 - 2 * core, q))

    @pl.when(p < 2)
    def _():
        xb_own().wait()
        xb_pair().start()
        for o in (0, 2, 1):
            xb_copy(o).start()

    def streams(k):
        for r, t, lg, clg, kids in info:
            n = k - lg
            other = q != r

            @pl.when((n >= 0) & (n < ND) & other)
            def _():
                hop(r, t, n, 0).wait_recv()
                for d in range(4):
                    pl.when(kids[d] == 1)(lambda d=d: hop(r, t, n, d).start())

            @pl.when((k == clg) & other)
            def _():
                com_hop(r, t, 0).wait_recv()
                for d in range(4):
                    pl.when(kids[d] == 1)(lambda d=d: com_hop(r, t, d).start())

    def rz_copy(o):
        return rcopy(rz.at[z], rz.at[z], s_rzs.at[o], s_rzr.at[z], (p, zm[o]))

    def ev_y():
        for o in range(1, 4):
            src = (y + o) % 4
            rcopy(ry.at[src], ry.at[src], s_rys.at[0], s_ryr.at[src], (p, ym[0])).wait_recv()
        rz[z] = ((ry[0] + ry[1]) + (ry[2] + ry[3]))
        for o in (3, 4, 2, 5, 1, 6, 0):
            rz_copy(o).start()

    def ev_z():
        for o in range(1, 8):
            src = (z + o) % 8
            rcopy(rz.at[src], rz.at[src], s_rzs.at[0], s_rzr.at[src], (p, zm[0])).wait_recv()
        tot = rz[0]
        for k in range(1, 8):
            tot = tot + rz[k]
        for i in range(4):
            res_ref[i] = rhs_ref[i] - row_of(tot[4 * i : 4 * i + 4, :])

        @pl.when(is_q)
        def _():
            acc[0:1, :] = res_ref[0]

    def x_copy(j, o):
        return rcopy(xs.at[j], xs.at[j], s_xss.at[o], s_xsr.at[j], ((j + o) % 8, 0))

    def x_recv(j):
        rcopy(xs.at[j], xs.at[j], s_xss.at[0], s_xsr.at[j], ((p + 1) % 8, 0)).wait_recv()

    def ev_c(j):
        @pl.when(is_q & (p > j))
        def _():
            rcopy(a_v.at[pl.ds(0, B)], chb.at[j], s_blks, s_blkr.at[j], ((p + 1) % 8, 0)).wait_recv()
            x_recv(j)
            row = row_of(xs[j, 0:4, :]).astype(bf16)
            acc[0:1, :] = acc[0:1, :] - dot_t(jnp.broadcast_to(row, (16, B)), chb[j])[0:1, :]

        @pl.when(is_q & (p == j))
        def _():
            s = acc[0:1, :]
            hi = s.astype(bf16).astype(f32)
            mid = (s - hi).astype(bf16).astype(f32)
            lo = (s - hi - mid).astype(bf16).astype(f32)
            k = lax.broadcasted_iota(jnp.int32, (16, B), 0)
            lhs = jnp.where(k == 0, hi, jnp.where(k == 1, mid, jnp.where(k == 2, lo, 0.0)))
            r3 = dot_t(lhs.astype(bf16), inv_v[...])
            x = (r3[0:1, :] + r3[1:2, :]) + r3[2:3, :]
            for m in range(4):
                xs[j, m : m + 1, :] = x[:, 128 * m : 128 * (m + 1)]
            xs[j, 4:8, :] = jnp.zeros((4, 128), f32)
            for o in (1, 2, 3, 4, 5, 6, 7):
                x_copy(j, o).start()

    def fz_copy(o):
        return rcopy(pk, pk, s_fs.at[o], s_fz, (p, zm[o]))

    def fy_copy(o):
        return rcopy(pk, pk, s_fs.at[7 + o], s_fy, (p, ym[o]))

    def ev_f0():
        @pl.when(is_q)
        def _():
            for j in range(8):
                pl.when(p < j)(lambda j=j: x_recv(j))
            for j in range(8):
                pk[4 * j : 4 * j + 4, :] = xs[j, 0:4, :]
            for o in (3, 4, 2, 5, 1, 6, 0):
                fz_copy(o).start()
            for o in range(3):
                fy_copy(o).start()

    def ev_f1():
        @pl.when((y == 0) & (z != 0))
        def _():
            fz_copy(0).wait_recv()
            for o in range(3):
                fy_copy(o).start()

    def ev_f2():
        pl.when(y != 0)(lambda: fy_copy(0).wait_recv())
        for j in range(8):
            pre_ref[j : j + 1, :] = row_of(pk[4 * j : 4 * j + 4, :])

    def ev_x():
        @pl.when(p >= 2)
        def _():
            rcopy(xb.at[core], xb.at[core], s_xsend.at[0], s_prim, (p, nbr[0])).wait_recv()
            xb_pair().start()

        rcopy(xb.at[1 - core], xb.at[1 - core], s_xsend.at[0], s_oth, (p, nbr[0])).wait_recv()
        v_f[...] = dot(u_v[0], dot(l_v[0], xb[0]).astype(bf16))

    half = pl.ds(pl.multiple_of(256 * core, 256), 256)

    def g_copy(r, o):
        return rcopy(
            strm.at[r, pl.ds(4 * B, 64)], comf.at[r, piece(p)], s_gs.at[r, o], s_gr.at[r, p // 2], (pm[2 * o + 1], q)
        )

    def c_copy(r):
        return rcopy(comf.at[r, half], comf.at[r, half], s_cs.at[r], s_cr.at[r], (p + 1 - 2 * core, q))

    def ev_com():
        for r in range(2):
            for o in range(3):
                g_copy(r, o).start()
            comf[r, piece(p)] = strm[r, 4 * B : 4 * B + 64]

    def ev_pair():
        for r in range(2):
            for o in range(3):
                src = pm[2 * o + 1]
                rcopy(
                    strm.at[r, pl.ds(4 * B, 64)], comf.at[r, piece(src)], s_gs.at[r, o], s_gr.at[r, src // 2], (src, q)
                ).wait_recv()
            c_copy(r).start()

    def ev_w():
        for r in range(2):
            other = comf.at[r, pl.ds(pl.multiple_of(256 - 256 * core, 256), 256)]
            rcopy(other, other, s_cs.at[r], s_cr.at[r], (p + 1 - 2 * core, q)).wait_recv()
        v = v_f[...]
        d = (xb[1].astype(f32) - dot(comf[0], v.astype(bf16))).astype(bf16)
        w1 = dot(u_v[1], dot(l_v[1], d).astype(bf16)).astype(bf16)
        w_v[1] = w1
        v1 = dot(u_v[0], dot(l_v[0], comf[1]).astype(bf16)).astype(bf16)
        w_v[0] = (v - dot(v1, w1)).astype(bf16)

    def com_ready():
        for r in range(2):
            pl.when((q == r) & jnp.logical_not(src_com))(lambda r=r: com_copy(0).wait_recv())
        for r in range(2):
            pl.when(q == r)(lambda r=r: [com_hop(r, t, ROOT_DIR[r][t]).start() for t in range(4)] and None)
        inject(NPOS, ND)

    com_ready()
    events = ((EY, ev_y), (EZ, ev_z), (EX, ev_x), (EF0, ev_f0), (EF1, ev_f1))

    def tick(k, c):
        for when, ev in events:
            pl.when(k == when)(ev)
        pl.when((k >= EC) & ((k - EC) % ECS == 0) & (k < EC + 8 * ECS))(lambda: ev_c((k - EC) // ECS))
        pl.when(k == com_tick)(ev_com)
        pl.when(k == com_tick + PD)(ev_pair)
        pl.when(k == w_tick)(ev_w)
        streams(k)
        return c

    lax.fori_loop(0, LAST, tick, 0)

    def step(s, c):
        i256 = pl.ds(pl.multiple_of(s * B, B), B)
        prod = dot(strm[0, i256], w_v[0]) + dot(strm[1, i256], w_v[1])
        out_v[i256] = (a_v[i256].astype(f32) - prod).astype(bf16)
        pltpu.make_async_copy(out_v.at[i256], out_hbm.at[i256], s_out).start()
        return c

    lax.fori_loop(0, 4, step, 0)
    ev_f2()

    for r, t, lg, clg, kids in info:
        for d in range(4):
            sent = strm.at[r, pl.ds(0, B + CR)]
            pl.when(kids[d] == 1)(
                lambda r=r, t=t, d=d, sent=sent: rcopy(sent, sent, s_send.at[r, t, d], s_recv.at[r, t, 0], (p, nbr[d])).wait_send()
            )
    for o in range(3):
        ry_copy(o).wait_send()
    for o in range(7):
        rz_copy(o).wait_send()

    @pl.when(src_com)
    def _():
        for o in range(7):
            com_copy(o).wait_send()

    for j in range(1, 7):
        pl.when((q == j) & (p > j))(lambda j=j: blk_copy(j).wait_send())
    xb_pair().wait_send()

    @pl.when(p < 2)
    def _():
        for o in range(3):
            xb_copy(o).wait_send()

    for r in range(2):
        c_copy(r).wait_send()
        for o in range(3):
            g_copy(r, o).wait_send()

    @pl.when(is_q)
    def _():
        for o in range(1, 8):
            x_copy(0, o).wait_send()
        for o in range(7):
            fz_copy(o).wait_send()

    @pl.when(y == 0)
    def _():
        for o in range(3):
            fy_copy(o).wait_send()

    pltpu.make_async_copy(out_v, out_hbm, s_out).wait()


def hand_out(a_hbm, res_in, pre_in, out_hbm, res_out, pre_out, buf, res_v, pre_v, s_in, s_out):
    steps = [(a_hbm.at[w], buf.at[w], out_hbm.at[w]) for w in (pl.ds(256 * k, 256) for k in range(8))]
    steps = [(res_in, res_v, res_out), (pre_in, pre_v, pre_out)] + steps
    ins = [pltpu.make_async_copy(a, b, s_in.at[k]) for k, (a, b, c) in enumerate(steps)]
    outs = [pltpu.make_async_copy(b, c, s_out.at[k]) for k, (a, b, c) in enumerate(steps)]
    for c in ins:
        c.start()
    for c, o in zip(ins, outs):
        c.wait()
        o.start()
    for o in outs:
        o.wait()


def shards(matrix, upper_inv, lower_inv, solution, right_side, diagonal_block_inverses):
    dma, vm = pltpu.SemaphoreType.DMA, pltpu.VMEM
    hbm = pl.BlockSpec(memory_space=pl.ANY)
    vmem = pl.BlockSpec(memory_space=pltpu.VMEM)
    updated, residual, precond = pl.pallas_call(
        kernel,
        out_shape=(
            jax.ShapeDtypeStruct((4 * B, B), bf16),
            jax.ShapeDtypeStruct((4, 1, B), f32),
            jax.ShapeDtypeStruct((8, B), f32),
        ),
        in_specs=[hbm, hbm, hbm, vmem, vmem, hbm],
        out_specs=(hbm, vmem, vmem),
        scratch_shapes=[
            vm((4 * B, B), bf16), vm((2, 4 * B + 64, B), bf16), vm((2, B, B), bf16), vm((2, B, B), bf16),
            vm((B, B), bf16), vm((7, B, B), bf16), vm((2, B, B), bf16), vm((2, B, B), bf16), vm((2, B, B), bf16),
            vm((B, B), f32), vm((4, 16, 128), f32), vm((8, 16, 128), f32), vm((8, 8, 128), f32), vm((32, 128), f32), vm((8, B), f32),
            vm((4 * B, B), bf16),
            dma((7,)), dma, dma((2, 4, 4)), dma((2, 4, ND + 1)), dma((4,)), dma, dma, dma((7,)), dma,
            dma, dma((7,)), dma((3,)), dma((4,)), dma((7,)), dma((8,)), dma((8,)), dma((8,)), dma((10,)), dma, dma,
            dma((2,)), dma((2,)), dma((2, 3)), dma((2, 4)),
        ],
        compiler_params=pltpu.CompilerParams(collective_id=0, has_side_effects=True, vmem_limit_bytes=56 << 20),
        cost_estimate=pl.CostEstimate(flops=8 << 30, bytes_accessed=8 << 20, transcendentals=0),
    )(
        matrix.reshape(4 * B, B),
        upper_inv,
        lower_inv,
        solution.reshape(1, B),
        right_side,
        diagonal_block_inverses.reshape(B, B),
    )
    updated, residual, precond = pl.pallas_call(
        hand_out,
        out_shape=(
            jax.ShapeDtypeStruct((4 * B, B), bf16),
            jax.ShapeDtypeStruct((4, 1, B), f32),
            jax.ShapeDtypeStruct((8, B), f32),
        ),
        in_specs=[hbm, hbm, hbm],
        out_specs=(hbm, hbm, hbm),
        scratch_shapes=[vm((4 * B, B), bf16), vm((4, 1, B), f32), vm((8, B), f32), dma((10,)), dma((10,))],
        compiler_params=pltpu.CompilerParams(vmem_limit_bytes=60 << 20),
        cost_estimate=pl.CostEstimate(flops=0, bytes_accessed=4 << 20, transcendentals=0),
    )(updated, residual, precond)
    return updated.reshape(matrix.shape), residual, precond


def solution(mesh):
    return jax.shard_map(
        shards,
        mesh=mesh,
        in_specs=(
            P(None, "prow", None, None, "pcol", None),
            P(),
            P(),
            P(None, "pcol", None),
            P(None, "prow", None),
            P(None, "prow", None, None),
        ),
        out_specs=(P(None, "prow", None, None, "pcol", None), P(None, "prow", None), P()),
        check_vma=False,
    )
```
